128 devices in a mesh: dp: 32 (over x, z, core), tensor: 4 (over y).
Axes of the slice: x: 4, y: 4, z: 4, core: 2. Of those that a mesh axis runs over, the one named last changes fastest.
Arguments:
- hidden: bfloat16 [4096, 4096], P('dp', 'tensor'), may hold values from -6 to 6
- grad_out: bfloat16 [4096, 4096], P('dp', 'tensor'), may hold values from -0.59765625 to 0.59765625
- routes: int32 [4096, 8], P('dp'), may hold values from 0 to 63, all different within a row; in each aligned block of 128 rows (0 to 127, 128 to 255, ...) at most 20 rows name the same one
- route_probs: float32 [4096, 8], P('dp'), may hold values from 0.02 to 0.5
- w_gate: bfloat16 [64, 4096, 1536], P('dp', None, 'tensor'), may hold values from -0.09375 to 0.09375
- w_up: bfloat16 [64, 4096, 1536], P('dp', None, 'tensor'), may hold values from -0.09375 to 0.09375
- w_down: bfloat16 [64, 1536, 4096], P('dp', 'tensor'), may hold values from -0.15625 to 0.15625
- partner: int32 [32], replicated, may hold values from 0 to 31, as said below
- swap_count: int32 [32], replicated, may hold values from 1 to 64, as said below
Outputs:
- input_grad: bfloat16 [4096, 4096], P('dp', 'tensor')
- router_grad: bfloat16 [4096, 8], P('dp')
The draws below stay inside these ranges and needn't reach their ends.
Inputs may be any that keep to these rules, and one draw needn't show every extreme that they name: `routes`: each row names 8 different experts; within the 128 rows of one index of dp no expert is named by more than 20 rows, and in every draw some expert is named by exactly 20 rows there. A perfect matching: partner[partner[r]] = r and partner[r] != r; r and partner[r] differ in exactly one of their three lowest bits. `swap_count`: equal for both members of a matched pair; equal to 64 for some pair in every draw.
All inputs are finite; a program needn't handle non-finite values.
Results may differ from the reference program's by a relative error of at most 0.015.
Values may be sent and summed in bfloat16 or wider, within the bound.
A program may use at most 192 MiB of HBM per device.

```python
import math
import jax
import jax.numpy as jnp
import numpy as np
from jax import lax

D = 4096
FF = 1536
TOPK = 8
TOK_DEV = 128
EXPERTS = 64
CAP = 20
SWAP = 64
TOKENS = 4096
N_DP = 32
N_TENSOR = 4


def pair_ranks(key):
    offset = jax.random.randint(key, (), 0, 3)
    rank_number = jnp.arange(N_DP, dtype=jnp.int32)
    bit_number = (rank_number // 8 + offset) % 3
    return jnp.bitwise_xor(rank_number, jnp.left_shift(jnp.int32(1), bit_number)).astype(jnp.int32)


def draw_partner(key, part):
    return pair_ranks(key)


def draw_swap_count(key, part):
    partner_rank = pair_ranks(key)
    key = jax.random.fold_in(key, 7)
    count_key, pick_key = jax.random.split(key)
    rank_number = jnp.arange(N_DP, dtype=jnp.int32)
    drawn_counts = jax.random.randint(count_key, (N_DP,), 1, SWAP + 1)
    lower_rank = jnp.minimum(rank_number, partner_rank)
    counts_paired = drawn_counts[lower_rank]
    chosen = jax.random.randint(pick_key, (), 0, N_DP)
    chosen_low = jnp.minimum(chosen, partner_rank[chosen])
    return jnp.where(lower_rank == chosen_low, SWAP, counts_paired).astype(jnp.int32)


def level_of(rng, shape, cuts, low, largest):
    def one(dim, parts):
        heights = jax.random.uniform(jax.random.fold_in(jax.random.fold_in(rng, 6), dim), (parts,), jnp.float32, low / len(cuts), largest / len(cuts))
        return jnp.repeat(jnp.exp(heights), shape[dim] // parts).reshape((-1,) + (1,) * (len(shape) - dim - 1))

    loudness = one(*cuts[0])
    for cut in cuts[1:]:
        loudness = loudness * one(*cut)
    return loudness


def assign_block(own_key, own, number, rows, count, top, reach, lean):
    order = jax.random.permutation(own_key, count)
    crowded, common = load_shares(count, rows * top, reach, lean, True), load_shares(count, rows * top, reach, lean, False)
    places = jnp.arange(count)

    def named(tallies, turn):
        used = int((tallies > 0).sum())
        fixed = max(1, used // 4)
        shifted = fixed + (places - fixed + turn * (used - fixed)) % max(1, count - fixed)
        return jnp.zeros((count,), jnp.int32).at[order[jnp.where(places < fixed, places, shifted)]].set(jnp.asarray(tallies, jnp.int32))

    tallies = jnp.where(number % 4 == 0, named(crowded, number // 4), named(common, number - number // 4 - 1))
    mixed = jax.random.permutation(jax.random.fold_in(own, 3), count)
    donor, sink = mixed[0:count // 2 * 2:2], mixed[1:count // 2 * 2:2]
    room = jnp.minimum(tallies[donor] - 1, reach - tallies[sink]) // 2
    room = jnp.where((donor == order[0]) | (sink == order[0]) | (tallies[sink] == 0), 0, jnp.maximum(room, 0))
    shifted = jax.random.randint(jax.random.fold_in(own, 4), (count // 2,), 0, 1 << 20) % (room + 1)
    tallies = tallies.at[donor].add(-shifted).at[sink].add(shifted)
    members = jnp.searchsorted(jnp.cumsum(tallies), jnp.arange(rows * top), side="right").astype(jnp.int32)
    table = members.reshape(top, rows).T
    table = table[jax.random.permutation(jax.random.fold_in(own, 1), rows)]
    turn = jax.random.randint(jax.random.fold_in(own, 2), (rows, 1), 0, top)
    return jnp.take_along_axis(table, (jnp.arange(top)[None, :] + turn) % top, axis=1)


def load_shares(count, total, most, lean, full):
    loads = [(1 << 20) // math.isqrt(rank ** lean) + 1 for rank in range(1, count + 1)]
    largest = most if full else min(most, max(-(-total // count), total * loads[0] // sum(loads)))
    least = 1 if total - largest >= count - 1 else 0
    holding, spare = [largest] + [least] * (count - 1), total - largest - least * (count - 1)
    while spare > 0:
        free = [i for i in range(1, count) if holding[i] < largest] or [i for i in range(1, count) if holding[i] < most]
        pool, left = sum([loads[i] for i in free]), spare
        for i in free:
            extra = min(most - holding[i], max(1, left * loads[i] // pool), spare)
            holding[i] = holding[i] + extra
            spare = spare - extra
    return np.array(holding)


def scatter_about(rng, dims, deviation, limit, cuts=(), kind=jnp.bfloat16):
    gain = level_of(rng, dims, cuts, -0.22, 0.18) if cuts else 1.0
    array = jax.random.normal(rng, dims, jnp.float32) * deviation * gain
    return jnp.minimum(jnp.maximum(array, -limit), limit).astype(kind)


def setup_inputs(seed: int = 0) -> dict:
    splits = jax.random.split(jax.random.key(seed), 10)
    hidden = scatter_about(splits[0], (TOKENS, D), 1.0, 6.0, ((0, 32), (1, 4)))
    grad_out = scatter_about(splits[1], (TOKENS, D), 0.1, 0.59765625, ((0, 32), (1, 4)))
    routes_keys = jax.random.split(jax.random.fold_in(splits[2], 1), TOKENS // TOK_DEV)
    routes_turns = jax.random.permutation(jax.random.fold_in(splits[2], 3), TOKENS // TOK_DEV)
    routes = jax.vmap(lambda own, number: assign_block(jax.random.fold_in(splits[2], 2), own, number, TOK_DEV, EXPERTS, TOPK, CAP, 2))(routes_keys, routes_turns).reshape((TOKENS, TOPK))
    route_probs = jnp.clip(jnp.exp(math.log(0.5) - 3.218876 * jax.random.uniform(splits[3], (TOKENS, TOPK), jnp.float32) ** level_of(splits[3], (TOKENS, TOPK), ((0, 32),), -0.2, 0.2)), 0.02, 0.5)
    w_gate = scatter_about(splits[4], (EXPERTS, D, FF), D ** -0.5, 0.09375, ((0, 32), (2, 4)))
    w_up = scatter_about(splits[5], (EXPERTS, D, FF), D ** -0.5, 0.09375, ((0, 32), (2, 4)))
    w_down = scatter_about(splits[6], (EXPERTS, FF, D), FF ** -0.5, 0.15625, ((0, 32), (1, 4)))
    partner = draw_partner(jax.random.fold_in(splits[9], 71), 0)
    swap_count = draw_swap_count(jax.random.fold_in(splits[9], 71), 0)
    return {"hidden": hidden, "grad_out": grad_out, "routes": routes, "route_probs": route_probs, "w_gate": w_gate, "w_up": w_up, "w_down": w_down, "partner": partner, "swap_count": swap_count}


def slot_positions(route_row):
    onehot = (route_row[:, None] == jnp.arange(EXPERTS, dtype=jnp.int32)[None, :]).astype(jnp.int32)
    before = jnp.cumsum(onehot, axis=0) - onehot
    return jnp.sum(before * onehot, axis=1).astype(jnp.int32)


def reference(hidden, grad_out, routes, route_probs, w_gate, w_up, w_down, partner, swap_count):
    route_blocks = routes.reshape(N_DP, TOK_DEV * TOPK)
    position = jax.vmap(slot_positions)(route_blocks)
    source = jnp.arange(N_DP, dtype=jnp.int32)[:, None]
    slot_index = (route_blocks * (N_DP * CAP) + source * CAP + position).reshape(-1).astype(jnp.int32)
    pair_number = jnp.arange(TOKENS * TOPK, dtype=jnp.int32)
    slot_pairs = jnp.zeros((EXPERTS * N_DP * CAP,), jnp.int32).at[slot_index].set(pair_number)
    slot_mask = jnp.zeros((EXPERTS * N_DP * CAP,), jnp.float32).at[slot_index].set(1.0)
    flat_probs = route_probs.reshape(-1)
    block_width = FF // N_TENSOR

    def expert_step(totals, expert):
        input_total, prob_total = totals
        start = (expert * (N_DP * CAP)).astype(jnp.int32)
        pairs_here = lax.dynamic_slice_in_dim(slot_pairs, start, N_DP * CAP)
        mask_here = lax.dynamic_slice_in_dim(slot_mask, start, N_DP * CAP)
        owner_rows = pairs_here // TOPK
        mask_cast = mask_here.astype(hidden.dtype)[:, None]
        expert_in = hidden[owner_rows] * mask_cast
        expert_cot = grad_out[owner_rows] * mask_cast
        gate_matrix = w_gate[expert]
        up_matrix = w_up[expert]
        down_matrix = w_down[expert]
        gate_pre = jnp.dot(expert_in, gate_matrix, preferred_element_type=jnp.float32)
        up_pre = jnp.dot(expert_in, up_matrix, preferred_element_type=jnp.float32)
        back_grad = jnp.dot(expert_cot, down_matrix.T, preferred_element_type=jnp.float32)
        sigmoid_gate = jax.nn.sigmoid(gate_pre)
        act = gate_pre * sigmoid_gate
        inner = act * up_pre
        slot_prob = jnp.sum(back_grad * inner, axis=1).astype(jnp.bfloat16)
        gate_grad = (back_grad * up_pre * sigmoid_gate * (1.0 + gate_pre * (1.0 - sigmoid_gate))).astype(jnp.bfloat16)
        up_grad = (back_grad * act).astype(jnp.bfloat16)
        slot_total = jnp.zeros((N_DP * CAP, D), jnp.float32)
        for piece_number in range(N_TENSOR):
            low_edge = piece_number * block_width
            high_edge = low_edge + block_width
            partial_sum = jnp.dot(gate_grad[:, low_edge:high_edge], gate_matrix[:, low_edge:high_edge].T, preferred_element_type=jnp.float32)
            partial_sum = partial_sum + jnp.dot(up_grad[:, low_edge:high_edge], up_matrix[:, low_edge:high_edge].T, preferred_element_type=jnp.float32)
            rounded = lax.optimization_barrier(partial_sum.astype(jnp.bfloat16))
            slot_total = slot_total + rounded.astype(jnp.float32)
        slot_grad = slot_total.astype(jnp.bfloat16)
        scale = flat_probs[pairs_here] * mask_here
        input_total = input_total.at[owner_rows].add(scale[:, None] * slot_grad.astype(jnp.float32))
        prob_total = prob_total.at[pairs_here].add(slot_prob.astype(jnp.float32) * mask_here)
        return (input_total, prob_total), None

    initial = (jnp.zeros((TOKENS, D), jnp.float32), jnp.zeros((TOKENS * TOPK,), jnp.float32))
    totals, _ = lax.scan(expert_step, initial, jnp.arange(EXPERTS, dtype=jnp.int32))
    input_total, prob_total = totals
    owner_grad = input_total.astype(jnp.bfloat16).reshape(N_DP, TOK_DEV, D)
    partner_grad = owner_grad[partner]
    row_number = jnp.arange(TOK_DEV, dtype=jnp.int32)
    taken = row_number[None, :] >= (TOK_DEV - swap_count)[:, None]
    input_grad = jnp.where(taken[:, :, None], partner_grad, owner_grad).reshape(TOKENS, D)
    router_grad = prob_total.astype(jnp.bfloat16).reshape(TOKENS, TOPK)
    return (input_grad, router_grad)
```

```python
import functools
import jax
import jax.numpy as jnp
from jax import lax
from jax.experimental import pallas as pl
from jax.experimental.pallas import tpu as pltpu
from jax.sharding import PartitionSpec as P

MESH = pl.DeviceIdType.MESH
BF=jnp.bfloat16; F32=jnp.float32
OROWS=144
HA=640
GA=512
CA=HA+GA
CQ=2048-CA
STEPS=(0,-1,1,2)
CHIPS=((0,0),(0,-1),(-1,0),(-1,-1),(0,1),(1,0),(-1,1),(1,-1),(1,1),(0,2),(2,0),(-1,2),(2,-1),(1,2),(2,1),(2,2))
PR=48
ORDERS=(("x","y","z"),("y","z","x"),("z","x","y"))
JS=(2,1,-1,0)

def nt(a,b): return lax.dot_general(a,b,(((1,),(1,)),((),())),preferred_element_type=F32)
def nn(a,b): return jnp.dot(a,b,preferred_element_type=F32)

def expert_kernel(hid, gra, ext, wg_hbm, wu_hbm, wd_hbm, D, gq, wg, wu, wd, xh, xg, ga, ex, rs, rr, onehot, prob, sprob, qb,
                  gate, up, back, gg, ug, spt, own_sem, wsem, qsem, dsem, send_sem, recv_sem):
    dp = lax.axis_index("dp"); y = lax.axis_index("tensor")
    x = dp // 8; z = (dp // 2) % 4; c = dp % 2
    here = {"x": x, "y": y, "z": z}
    def device(axis, step):
        if axis == "c":
            return {"dp": x * 8 + z * 2 + (1 - c), "tensor": y}
        at = dict(here)
        at[axis] = (at[axis] + step + 4) % 4
        return {"dp": at["x"] * 8 + at["z"] * 2 + c, "tensor": at["y"]}
    barrier = pltpu.get_barrier_semaphore()
    partners = [device(a, s) for a in "xyz" for s in (1, -1)] + [device("c", 0)]
    for p in partners:
        pl.semaphore_signal(barrier, inc=1, device_id=p, device_id_type=MESH)
    pl.semaphore_wait(barrier, len(partners))

    number = [0]
    pending = []
    def send(src, dst, to):
        n = number[0]; number[0] += 1
        copy = pltpu.make_async_remote_copy(src_ref=src, dst_ref=dst, send_sem=send_sem.at[n],
            recv_sem=recv_sem.at[n], device_id=to, device_id_type=MESH)
        copy.start()
        pending.append(copy)
        return copy
    mine = [pltpu.make_async_copy(a, b, own_sem.at[i]) for i, (a, b) in enumerate((
        (ext, ex.at[x, z, c]),
        (hid.at[:, pl.ds(0, HA)], ga.at[x, z, c, :, pl.ds(0, HA)]),
        (gra.at[:, pl.ds(0, GA)], ga.at[x, z, c, :, pl.ds(HA, GA)]),
        (hid.at[:, pl.ds(HA, 1024 - HA)], gq.at[x, z, c, y, :, pl.ds(0, 1024 - HA)]),
        (gra.at[:, pl.ds(GA, 1024 - GA)], gq.at[x, z, c, y, :, pl.ds(1024 - HA, 1024 - GA)])))]
    for m in mine: m.start()
    for m in mine: m.wait()

    def view(fam, at, part="all"):
        xx = pl.ds(0, 4) if at["x"] is None else at["x"]
        if fam == "E":
            return ex.at[xx, at["z"], c]
        if fam in ("alo", "ahi"):
            first = 0 if fam == "alo" else 64
            first, count = {"all": (first, 64), "up": (first, 32), "down": (first + 32, 32)}[part]
            return ga.at[xx, at["z"], c, pl.ds(first, count)]
        if fam in ("qlo", "qhi"):
            ys = {"all": pl.ds(0, 4), "up": pl.ds(0, 2), "down": pl.ds(2, 2)}[part]
            return gq.at[xx, at["z"], c, ys, pl.ds(0 if fam == "qlo" else 64, 64)]
        rows = {"all": (0, 128), "up": (0, 64), "down": (64, 64)}[part]
        return gq.at[x, z, c, at["y"], pl.ds(*rows)]
    sibs = {}
    def to_sibling(fam, at, key):
        if key is None: return
        v = view(fam, at)
        sibs[(fam,) + key] = send(v, v, device("c", 0))
    def moved(at, axis, step):
        q = dict(at); q[axis] = (here[axis] + step + 4) % 4
        return q
    class Ring:
        def __init__(self, fam, axis, at, off):
            self.fam, self.axis, self.at, self.off = fam, axis, at, off
            v = view(fam, at)
            self.up = send(v, v, device(axis, 1))
            self.down = send(v, v, device(axis, -1))
        def key(self, step):
            if self.off is None: return None
            o = dict(self.off); o[self.axis] = step
            return (o["x"], o["z"])
        def forward(self):
            f, a = self.fam, self.axis
            before, after = moved(self.at, a, -1), moved(self.at, a, 1)
            self.up.wait_recv()
            v = view(f, before, "up")
            self.up2 = send(v, v, device(a, 1))
            to_sibling(f, before, self.key(-1))
            self.down.wait_recv()
            self.down2 = None
            if f != "E":
                v = view(f, after, "down")
                self.down2 = send(v, v, device(a, -1))
            to_sibling(f, after, self.key(1))
        def finish(self):
            self.up2.wait_recv()
            if self.down2 is not None: self.down2.wait_recv()
            to_sibling(self.fam, moved(self.at, self.axis, 2), self.key(2))
    def sets(q):
        return ((q + "lo", "x", "z"), (q + "hi", "z", "x"))
    R = {}
    zero = {"x": 0, "z": 0}
    def stage_one(q):
        for f, a, b in sets(q): R[f, 1] = Ring(f, a, here, zero)
        for f, a, b in sets(q): R[f, 2, 0] = Ring(f, b, here, zero)
        for f, a, b in sets(q): to_sibling(f, here, (0, 0))
    def stage_two(q, steps):
        for f, a, b in sets(q):
            for s in steps:
                off = dict(zero); off[a] = s
                R[f, 2, s] = Ring(f, b, moved(here, a, s), off)
    def forward(q, *which):
        for f, a, b in sets(q): R[(f,) + which].forward()
    def finish(q, *which):
        for f, a, b in sets(q): R[(f,) + which].finish()

    e1 = Ring("E", "x", here, zero)
    qy = Ring("Q", "y", here, None)
    stage_one("a")
    to_sibling("E", here, (0, 0))
    weights = [pltpu.make_async_copy(a, b, wsem.at[i]) for i,(a,b) in enumerate(((wg_hbm,wg),(wu_hbm,wu),(wd_hbm,wd)))]
    e1.forward()
    forward("a", 1)
    stage_two("a", (-1, 1))
    e1.finish()
    def e_sib(step):
        at = moved(here, "z", step); at["x"] = None
        v = view("E", at)
        sibs["E", "col", step] = send(v, v, device("c", 0))
    col = dict(here); col["x"] = None
    e2 = Ring("E", "z", col, None)
    finish("a", 1)
    stage_two("a", (2,))
    qy.forward()
    e2.forward()
    e_sib(-1); e_sib(1)
    forward("a", 2, 0)
    qy.finish()
    stage_one("q")
    e2.finish()
    e_sib(2)
    for w in weights: w.start()
    for k in ((0, 0), (-1, 0), (1, 0), (2, 0)): sibs[("E",) + k].wait_recv()
    for s in (-1, 1, 2): sibs["E", "col", s].wait_recv()

    place = [((x + dx + 4) % 4, (z + dz + 4) % 4) for dx, dz in CHIPS]
    for n, (px, pz) in enumerate(place):
        for s in range(2):
            block = ex[px, pz, s].astype(F32)
            for q in range(3):
                rs[q, 2 * n + s:2 * n + s + 1, :] = block[q:q + 1]
    routes = [rs[0, :, k * 128:(k + 1) * 128] for k in range(8)]
    probs = [rs[1, :, k * 128:(k + 1) * 128] + rs[2, :, k * 128:(k + 1) * 128] for k in range(8)]
    tri = (lax.broadcasted_iota(jnp.int32, (128, 128), 0) < lax.broadcasted_iota(jnp.int32, (128, 128), 1)).astype(F32).astype(BF)
    for e in range(2):
        name = (dp * 2 + e).astype(F32)
        member = jnp.zeros((32, 128), F32); weight = jnp.zeros((32, 128), F32)
        for k in range(8):
            hit = routes[k] == name
            member = member + jnp.where(hit, 1.0, 0.0)
            weight = weight + jnp.where(hit, probs[k], 0.0)
        before = nn(member.astype(BF), tri)
        offset = ((lax.broadcasted_iota(jnp.int32, (32, 128), 0) % 4) * 20).astype(F32)
        target = jnp.where(member > 0.5, before + offset, -1.0)
        for g in range(8):
            t4 = jnp.concatenate([target[g * 4 + i:g * 4 + i + 1] for i in range(4)], axis=1)
            w4 = jnp.concatenate([weight[g * 4 + i:g * 4 + i + 1] for i in range(4)], axis=1)
            oh = jnp.where(lax.broadcasted_iota(jnp.int32, (80, 512), 0).astype(F32) == t4, 1.0, 0.0)
            onehot[g, e * 80:(e + 1) * 80, :] = oh.astype(BF)
            prob[e, g * 80:(g + 1) * 80, :] = jnp.broadcast_to(jnp.sum(oh * w4, axis=1, keepdims=True), (80, 128))

    waited = set()
    def need(q, g):
        for key in CHIPS[2 * g:2 * g + 2]:
            for f, a, b in sets(q):
                if (f, key) not in waited:
                    waited.add((f, key))
                    sibs[(f,) + key].wait_recv()
    base = pl.multiple_of(y * 1024, 1024)
    def pack_own(g):
        need("a", g)
        v = jnp.concatenate([ga[px, pz].reshape(256, CA) for px, pz in place[2 * g:2 * g + 2]], axis=0)
        out = nn(onehot[g], v).astype(BF)
        rows = pl.ds(g * 80, 80)
        for e in range(2):
            xh[e, rows, pl.ds(base, HA)] = out[e * 80:(e + 1) * 80, :HA]
            xg[e, rows, pl.ds(base, GA)] = out[e * 80:(e + 1) * 80, HA:]
    class Slots:
        def __init__(self, g):
            self.g = g
            self.up = [send(v, v, device("y", 1)) for v in self.refs(y)]
            self.down = [send(v, v, device("y", -1)) for v in self.refs(y)]
        def refs(self, yy, es=pl.ds(0, 2)):
            at = pl.multiple_of(yy * 1024, 1024)
            rows = pl.ds(self.g * 80, 80)
            return xh.at[es, rows, pl.ds(at, HA)], xg.at[es, rows, pl.ds(at, GA)]
        def forward(self):
            for w in self.up: w.wait_recv()
            self.up2 = [send(v, v, device("y", 1)) for v in self.refs((y + 3) % 4, pl.ds(0, 1))]
            for w in self.down: w.wait_recv()
            self.down2 = [send(v, v, device("y", -1)) for v in self.refs((y + 1) % 4, pl.ds(1, 1))]
        def finish(self):
            for w in self.up2 + self.down2: w.wait_recv()
            for w in self.up + self.down + self.up2 + self.down2:
                w.wait_send()
                pending[:] = [q for q in pending if q is not w]
    def q_copies(g, yy):
        return [pltpu.make_async_copy(gq.at[px, pz, :, yy], qb.at[yy, i], qsem.at[yy, i])
                for i, (px, pz) in enumerate(place[2 * g:2 * g + 2])]
    def q_start(g):
        for yy in range(4):
            for w in q_copies(g, yy): w.start()
    def pack_rest(groups):
        for g in groups: need("q", g)
        q_start(groups[0])
        for g, after in zip(groups, groups[1:] + (None,)):
            for yy in range(4):
                for w in q_copies(g, yy): w.wait()
                out = nn(onehot[g], qb[yy].reshape(512, CQ)).astype(BF)
                rows = pl.ds(g * 80, 80)
                for e in range(2):
                    xh[e, rows, yy * 1024 + HA:(yy + 1) * 1024] = out[e * 80:(e + 1) * 80, :1024 - HA]
                    xg[e, rows, yy * 1024 + GA:(yy + 1) * 1024] = out[e * 80:(e + 1) * 80, 1024 - HA:]
                if after is not None:
                    for w in q_copies(after, yy): w.start()
    def hidden_units(h, e):
        rows = pl.ds(h * 320, 320)
        gate[...] = jnp.zeros_like(gate); up[...] = jnp.zeros_like(up); back[...] = jnp.zeros_like(back)
        @pl.loop(0, 8)
        def _(kk):
            cols = pl.ds(pl.multiple_of(kk * 512, 512), 512)
            a = xh[e, rows, cols]
            gate[...] += nn(a, wg[e, cols, :])
            up[...] += nn(a, wu[e, cols, :])
            back[...] += nt(xg[e, rows, cols], wd[e, :, cols])
        @pl.loop(0, 4)
        def _(r):
            here_rows = pl.ds(pl.multiple_of(r * 80, 16), 80)
            all_rows = pl.ds(pl.multiple_of(h * 320 + r * 80, 16), 80)
            gp = gate[here_rows, :]; u = up[here_rows, :]; b = back[here_rows, :]
            sig = 1.0 / (1.0 + jnp.exp(-gp))
            act = gp * sig
            sprob[e, all_rows, :] = jnp.broadcast_to(jnp.sum(b * act * u, axis=1, keepdims=True), (80, 128))
            p = prob[e, all_rows, 0:1]
            gg[here_rows, :] = (b * u * sig * (1.0 + gp * (1.0 - sig)) * p).astype(BF)
            ug[here_rows, :] = (b * act * p).astype(BF)
        @pl.loop(0, 8)
        def _(kk):
            cols = pl.ds(pl.multiple_of(kk * 512, 512), 512)
            xh[e, rows, cols] = (nt(gg[...], wg[e, cols, :]) + nt(ug[...], wu[e, cols, :])).astype(BF)

    S = {}
    forward("a", 2, -1)
    pack_own(0); S[0] = Slots(0)
    pack_own(1); S[1] = Slots(1)
    forward("a", 2, 1)
    pack_own(2); S[2] = Slots(2)
    pack_own(3)
    forward("a", 2, 2)
    for s in STEPS: finish("a", 2, s)
    for g in range(4, 8): pack_own(g)
    S[0].forward(); S[3] = Slots(3)
    S[1].forward(); S[4] = Slots(4)
    forward("q", 1)
    stage_two("q", (-1, 1))
    S[2].forward(); S[5] = Slots(5)
    forward("q", 2, 0)
    finish("q", 1)
    stage_two("q", (2,))
    S[3].forward(); S[6] = Slots(6)
    forward("q", 2, -1)
    pack_rest((0, 1))
    S[4].forward(); S[7] = Slots(7)
    forward("q", 2, 1)
    pack_rest((2, 3))
    for w in weights: w.wait()
    for g in range(4): S[g].finish()
    hidden_units(0, 0)
    S[5].forward()
    finish("q", 2, 0)
    forward("q", 2, 2)
    hidden_units(0, 1)
    S[6].forward()
    finish("q", 2, -1)
    finish("q", 2, 1)
    S[7].forward()
    finish("q", 2, 2)
    pack_rest((4, 5, 6, 7))
    for g in range(4, 8): S[g].finish()
    for e in range(2): hidden_units(1, e)
    for s in pending: s.wait_send()

    for g in range(8):
        for e in range(2):
            oh = onehot[g, e * 80:(e + 1) * 80, :].astype(F32)
            row = jnp.sum(oh * sprob[e, g * 80:(g + 1) * 80, 0:1], axis=0, keepdims=True)
            for i in range(4):
                spt[e, g * 4 + i:g * 4 + i + 1, :] = row[:, i * 128:(i + 1) * 128]
    n0 = (dp * 2).astype(F32)
    first = lax.broadcasted_iota(jnp.int32, (32, 16, 128), 1) == 0
    for k in range(8):
        r = rs[0, :, k * 128:(k + 1) * 128]
        v = jnp.where(r == n0, spt[0], 0.0) + jnp.where(r == n0 + 1.0, spt[1], 0.0)
        rr[:, :, k * 128:(k + 1) * 128] = jnp.where(first, v[:, None, :], 0.0).astype(BF)

    def d_copies(g, t):
        s = t % 2
        return [pltpu.make_async_copy(xg.at[s, pl.ds(i * OROWS, OROWS), pl.ds(0, 1024)],
                    D.at[t, place[2 * g + i // 2][0], place[2 * g + i // 2][1], i % 2], dsem.at[s, i]) for i in range(4)]
    for g in range(8):
        oht = onehot[g].astype(F32).T.astype(BF)
        for t in range(4):
            n = g * 4 + t
            if n >= 2:
                for w in d_copies((n - 2) // 4, (n - 2) % 4): w.wait()
            v = jnp.concatenate([xh[e, g * 80:(g + 1) * 80, t * 1024:(t + 1) * 1024] for e in range(2)], axis=0)
            out = nn(oht, v).astype(BF)
            for i in range(4):
                xg[t % 2, i * OROWS:i * OROWS + 128, 0:1024] = out[i * 128:(i + 1) * 128]
                xg[t % 2, i * OROWS + 128:(i + 1) * OROWS, 0:1024] = rr[g * 4 + i]
            for w in d_copies(g, t): w.start()
    for n in (30, 31):
        for w in d_copies(n // 4, n % 4): w.wait()

def experts(hid, gra, ext, wg, wu, wd):
    V=pltpu.VMEM
    A=pl.BlockSpec(memory_space=pl.ANY)
    N=4 + 3 + 7 + 4 + 2 * (40 + 32) + 64
    return pl.pallas_call(expert_kernel,
        out_shape=(jax.ShapeDtypeStruct((4,4,4,2,OROWS,1024),BF), jax.ShapeDtypeStruct((4,4,2,4,128,CQ),BF)),
        in_specs=[A]*6, out_specs=(A,A),
        scratch_shapes=[V((2,4096,384),BF),V((2,4096,384),BF),V((2,384,4096),BF),
            V((2,640,4096),BF),V((2,640,4096),BF),V((4,4,2,128,CA),BF),V((4,4,2,16,1024),BF),V((3,32,1024),F32),V((32,16,1024),BF),
            V((8,160,512),BF),V((2,640,128),F32),V((2,640,128),F32),V((4,2,2,128,CQ),BF),
            V((320,384),F32),V((320,384),F32),V((320,384),F32),V((320,384),BF),V((320,384),BF),V((2,32,128),F32),
            pltpu.SemaphoreType.DMA((5,)),pltpu.SemaphoreType.DMA((3,)),pltpu.SemaphoreType.DMA((4,2)),pltpu.SemaphoreType.DMA((2,4)),
            pltpu.SemaphoreType.DMA((N,)),pltpu.SemaphoreType.DMA((N,))],
        compiler_params=pltpu.CompilerParams(collective_id=0, has_side_effects=True, vmem_limit_bytes=63*1024*1024),
    )(hid, gra, ext, wg, wu, wd)[0]

def return_kernel(D, pick, grad, router, sib, own, r1, r2, r3, m2, m3, fin, inc, own_sem, send_sem, recv_sem):
    dp = lax.axis_index("dp"); y = lax.axis_index("tensor")
    x = dp // 8; z = (dp // 2) % 4; c = dp % 2
    here = {"x": x, "y": y, "z": z}
    def device(axis, step):
        if axis == "c":
            return {"dp": x * 8 + z * 2 + (1 - c), "tensor": y}
        at = dict(here)
        at[axis] = (at[axis] + step + 4) % 4
        return {"dp": at["x"] * 8 + at["z"] * 2 + c, "tensor": at["y"]}
    mates = []
    for bit in range(3):
        low = (dp // (1 << bit)) % 2
        mates.append({"dp": dp + (1 - 2 * low) * (1 << bit), "tensor": y})
    barrier = pltpu.get_barrier_semaphore()
    partners = [device(a, s) for a in "xyz" for s in (1, -1)] + mates
    for p in partners:
        pl.semaphore_signal(barrier, inc=1, device_id=p, device_id_type=MESH)
    pl.semaphore_wait(barrier, len(partners))

    number = [0]
    pending = []
    def send(src, dst, to):
        n = number[0]; number[0] += 1
        copy = pltpu.make_async_remote_copy(src_ref=src, dst_ref=dst, send_sem=send_sem.at[n],
            recv_sem=recv_sem.at[n], device_id=to, device_id_type=MESH)
        copy.start()
        pending.append(copy)
        return copy
    def block(p, j, k, core):
        A, B, C = ORDERS[p]
        at = {A: None, B: (here[B] + j + 4) % 4, C: (here[C] + k + 4) % 4}
        idx = tuple(pl.ds(0, 4) if at[a] is None else at[a] for a in "yxz")
        return D.at[idx + (core, pl.ds(p * PR, PR))]
    order = [(p, j, k) for j in JS for k in JS for p in range(3)]
    sibs = {}
    for p, j, k in order:
        sibs[p, j, k] = send(block(p, j, k, 1 - c), sib.at[p, JS.index(j), JS.index(k)], device("c", 0))
    NB = 6
    def own_copy(n):
        p, j, k = order[n]
        return pltpu.make_async_copy(block(p, j, k, c), own.at[n % NB], own_sem.at[n % NB])
    for n in range(NB): own_copy(n).start()
    def add(dst, *terms):
        @pl.loop(0, dst.shape[0])
        def _(i):
            total = terms[0][i].astype(F32)
            for t in terms[1:]: total = total + t[i].astype(F32)
            dst[i] = total.astype(BF)
    done = [0]
    def merge(p, j, k):
        n = done[0]; done[0] += 1
        assert order[n] == (p, j, k)
        own_copy(n).wait()
        sibs[p, j, k].wait_recv()
        m = sib.at[p, JS.index(j), JS.index(k)]
        add(m, m, own.at[n % NB])
        if n + NB < len(order): own_copy(n + NB).start()
        return m
    class Ring:
        def __init__(self, axis, land):
            self.axis, self.land = axis, land
        def start(self, far):
            a = self.axis
            self.up1 = send(far.at[0:2], self.land.at[0:2], device(a, 1))
            self.down1 = send(far.at[2:4], self.land.at[2:4], device(a, -1))
        def middle(self, after, before):
            a = self.axis
            self.up1.wait_recv()
            lo = after.at[0:2]
            add(lo, lo, self.land.at[0:2])
            self.up2 = send(after, self.land.at[4:8], device(a, 1))
            self.down1.wait_recv()
            hi = before.at[2:4]
            add(hi, hi, self.land.at[2:4])
            self.down2 = send(before, self.land.at[8:12], device(a, -1))
        def finish(self, near, out):
            self.up2.wait_recv(); self.down2.wait_recv()
            add(out, near, self.land.at[4:8], self.land.at[8:12])
    rings = {}
    M = {}
    def first(j):
        for k in JS:
            for p in range(3):
                M[p, j, k] = merge(p, j, k)
                if k == 2:
                    r = rings[p, j] = Ring(ORDERS[p][2], r1.at[p, JS.index(j)])
                    r.start(M[p, j, 2])
    def second(j):
        for p in range(3): rings[p, j].middle(M[p, j, 1], M[p, j, -1])
    def third(j):
        for p in range(3): rings[p, j].finish(M[p, j, 0], m2.at[p, JS.index(j)])
    late = {}
    first(2); first(1); second(2); first(-1); second(1); third(2)
    for p in range(3):
        late[p] = Ring(ORDERS[p][1], r2.at[p]); late[p].start(m2.at[p, 0])
    first(0); second(-1); third(1); second(0); third(-1)
    for p in range(3): late[p].middle(m2.at[p, 1], m2.at[p, 2])
    third(0)
    for p in range(3): late[p].finish(m2.at[p, 3], m3.at[p])
    last = {}
    cut = [pl.ds(0, 512), pl.ds(512, 512)]
    for p in range(3):
        A = ORDERS[p][0]
        far = m3.at[p, (here[A] + 2) % 4]
        last[p] = [send(far.at[:, cut[0]], r3.at[p, 0, :, cut[0]], device(A, 1)),
                   send(far.at[:, cut[1]], r3.at[p, 0, :, cut[1]], device(A, -1))]
    for p in range(3):
        A = ORDERS[p][0]
        for s in (0, 1):
            last[p][s].wait_recv()
            m = m3.at[p, (here[A] + (1, 3)[s]) % 4]
            m[:, cut[s]] = (m[:, cut[s]].astype(F32) + r3[p, 0, :, cut[s]].astype(F32)).astype(BF)
            last[p].append(send(m, r3.at[p, 1 + s], device(A, (1, -1)[s])))
    for p in range(3):
        A = ORDERS[p][0]
        last[p][2].wait_recv(); last[p][3].wait_recv()
        total = m3[p, here[A]].astype(F32) + r3[p, 1].astype(F32) + r3[p, 2].astype(F32)
        fin[p * PR:(p + 1) * PR, :] = total.astype(BF)
    swaps = [send(fin.at[64:128], inc.at[b], mates[b]) for b in range(3)]
    router[...] = fin[128:144, :]
    grad[0:64, :] = fin[0:64, :]
    for s in swaps: s.wait_recv()
    row = lax.broadcasted_iota(jnp.int32, (64, 1024), 0)
    kept = fin[64:128, :].astype(F32)
    taken = row >= 64 - pick[1]
    for b in range(3):
        kept = jnp.where(taken & (pick[0] == b), inc[b].astype(F32), kept)
    grad[64:128, :] = kept.astype(BF)
    for s in pending: s.wait_send()

def returned(D, pick):
    V=pltpu.VMEM
    N=48 + 3 * 4 * 4 + 3 * 4 + 3 * 4 + 3
    return pl.pallas_call(return_kernel,
        out_shape=(jax.ShapeDtypeStruct((128,1024),BF),jax.ShapeDtypeStruct((16,1024),BF)),
        in_specs=[pl.BlockSpec(memory_space=pl.ANY),pl.BlockSpec(memory_space=pltpu.SMEM)],
        out_specs=(pl.BlockSpec(memory_space=V),pl.BlockSpec(memory_space=V)),
        scratch_shapes=[V((3,4,4,4,PR,1024),BF),V((6,4,PR,1024),BF),V((3,4,12,PR,1024),BF),V((3,12,PR,1024),BF),
            V((3,3,PR,1024),BF),V((3,4,4,PR,1024),BF),V((3,4,PR,1024),BF),V((OROWS,1024),BF),V((3,64,1024),BF),
            pltpu.SemaphoreType.DMA((6,)),pltpu.SemaphoreType.DMA((N,)),pltpu.SemaphoreType.DMA((N,))],
        compiler_params=pltpu.CompilerParams(collective_id=1, has_side_effects=True, vmem_limit_bytes=62*1024*1024),
    )(D, pick)

def local(hidden, grad_out, routes, route_probs, w_gate, w_up, w_down, partner, swap_count):
    flat = route_probs.T.reshape(1, 1024)
    high = lax.reduce_precision(flat, 8, 7).astype(BF)
    low = (flat - high.astype(F32)).astype(BF)
    number = routes.T.reshape(1, 1024).astype(BF)
    ext = jnp.concatenate([number, high, low, jnp.zeros((13, 1024), BF)], axis=0)
    partial = experts(hidden, grad_out, ext, w_gate, w_up, w_down)
    rank = lax.axis_index("dp")
    apart = jnp.bitwise_xor(partner[rank], rank)
    pick = jnp.stack([apart // 2, swap_count[rank]]).astype(jnp.int32)
    grad, router = returned(partial, pick)
    return grad, router[0].reshape(8, 128).T


def solution(mesh):
    placed = (
        P("dp", "tensor"),
        P("dp", "tensor"),
        P("dp", None),
        P("dp", None),
        P("dp", None, "tensor"),
        P("dp", None, "tensor"),
        P("dp", "tensor", None),
        P(),
        P(),
    )
    return jax.shard_map(
        local,
        mesh=mesh,
        in_specs=placed,
        out_specs=(P("dp", "tensor"), P("dp", None)),
        check_vma=False,
    )
```

```python
import functools
import jax
import jax.numpy as jnp
from jax import lax
from jax.experimental import pallas as pl
from jax.experimental.pallas import tpu as pltpu
from jax.sharding import PartitionSpec as P

MESH = pl.DeviceIdType.MESH
BF=jnp.bfloat16; F32=jnp.float32
HA=640
GA=512
CA=HA+GA
CQ=2048-CA
STEPS=(0,-1,1,2)
CHIPS=((0,0),(0,-1),(-1,0),(-1,-1),(0,1),(1,0),(-1,1),(1,-1),(1,1),(0,2),(2,0),(-1,2),(2,-1),(1,2),(2,1),(2,2))
RA=512
RQ=1024-RA

def nt(a,b): return lax.dot_general(a,b,(((1,),(1,)),((),())),preferred_element_type=F32)
def nn(a,b): return jnp.dot(a,b,preferred_element_type=F32)

def expert_kernel(hid, gra, ext, wg_hbm, wu_hbm, wd_hbm, ws_out, oh_out, rr_out, gq, wg, wu, wd, xh, xg, ga, ex, rs, rr, onehot, prob, sprob, qb,
                  gate, up, back, gg, ug, spt, own_sem, wsem, qsem, send_sem, recv_sem):
    dp = lax.axis_index("dp"); y = lax.axis_index("tensor")
    x = dp // 8; z = (dp // 2) % 4; c = dp % 2
    here = {"x": x, "y": y, "z": z}
    def device(axis, step):
        if axis == "c":
            return {"dp": x * 8 + z * 2 + (1 - c), "tensor": y}
        at = dict(here)
        at[axis] = (at[axis] + step + 4) % 4
        return {"dp": at["x"] * 8 + at["z"] * 2 + c, "tensor": at["y"]}
    barrier = pltpu.get_barrier_semaphore()
    partners = [device(a, s) for a in "xyz" for s in (1, -1)] + [device("c", 0)]
    for p in partners:
        pl.semaphore_signal(barrier, inc=1, device_id=p, device_id_type=MESH)
    pl.semaphore_wait(barrier, len(partners))

    number = [0]
    pending = []
    def send(src, dst, to):
        n = number[0]; number[0] += 1
        copy = pltpu.make_async_remote_copy(src_ref=src, dst_ref=dst, send_sem=send_sem.at[n],
            recv_sem=recv_sem.at[n], device_id=to, device_id_type=MESH)
        copy.start()
        pending.append(copy)
        return copy
    mine = [pltpu.make_async_copy(a, b, own_sem.at[i]) for i, (a, b) in enumerate((
        (ext, ex.at[x, z, c]),
        (hid.at[:, pl.ds(0, HA)], ga.at[x, z, c, :, pl.ds(0, HA)]),
        (gra.at[:, pl.ds(0, GA)], ga.at[x, z, c, :, pl.ds(HA, GA)]),
        (hid.at[:, pl.ds(HA, 1024 - HA)], gq.at[x, z, c, y, :, pl.ds(0, 1024 - HA)]),
        (gra.at[:, pl.ds(GA, 1024 - GA)], gq.at[x, z, c, y, :, pl.ds(1024 - HA, 1024 - GA)])))]
    for m in mine: m.start()
    for m in mine: m.wait()

    def view(fam, at, part="all"):
        xx = pl.ds(0, 4) if at["x"] is None else at["x"]
        if fam == "E":
            return ex.at[xx, at["z"], c]
        if fam in ("alo", "ahi"):
            first = 0 if fam == "alo" else 64
            first, count = {"all": (first, 64), "up": (first, 32), "down": (first + 32, 32)}[part]
            return ga.at[xx, at["z"], c, pl.ds(first, count)]
        if fam in ("qlo", "qhi"):
            ys = {"all": pl.ds(0, 4), "up": pl.ds(0, 2), "down": pl.ds(2, 2)}[part]
            return gq.at[xx, at["z"], c, ys, pl.ds(0 if fam == "qlo" else 64, 64)]
        rows = {"all": (0, 128), "up": (0, 64), "down": (64, 64)}[part]
        return gq.at[x, z, c, at["y"], pl.ds(*rows)]
    sibs = {}
    def to_sibling(fam, at, key):
        if key is None: return
        v = view(fam, at)
        sibs[(fam,) + key] = send(v, v, device("c", 0))
    def moved(at, axis, step):
        q = dict(at); q[axis] = (here[axis] + step + 4) % 4
        return q
    class Ring:
        def __init__(self, fam, axis, at, off):
            self.fam, self.axis, self.at, self.off = fam, axis, at, off
            v = view(fam, at)
            self.up = send(v, v, device(axis, 1))
            self.down = send(v, v, device(axis, -1))
        def key(self, step):
            if self.off is None: return None
            o = dict(self.off); o[self.axis] = step
            return (o["x"], o["z"])
        def forward(self):
            f, a = self.fam, self.axis
            before, after = moved(self.at, a, -1), moved(self.at, a, 1)
            self.up.wait_recv()
            v = view(f, before, "up")
            self.up2 = send(v, v, device(a, 1))
            to_sibling(f, before, self.key(-1))
            self.down.wait_recv()
            self.down2 = None
            if f != "E":
                v = view(f, after, "down")
                self.down2 = send(v, v, device(a, -1))
            to_sibling(f, after, self.key(1))
        def finish(self):
            self.up2.wait_recv()
            if self.down2 is not None: self.down2.wait_recv()
            to_sibling(self.fam, moved(self.at, self.axis, 2), self.key(2))
    def sets(q):
        return ((q + "lo", "x", "z"), (q + "hi", "z", "x"))
    R = {}
    zero = {"x": 0, "z": 0}
    def stage_one(q):
        for f, a, b in sets(q): R[f, 1] = Ring(f, a, here, zero)
        for f, a, b in sets(q): R[f, 2, 0] = Ring(f, b, here, zero)
        for f, a, b in sets(q): to_sibling(f, here, (0, 0))
    def stage_two(q, steps):
        for f, a, b in sets(q):
            for s in steps:
                off = dict(zero); off[a] = s
                R[f, 2, s] = Ring(f, b, moved(here, a, s), off)
    def forward(q, *which):
        for f, a, b in sets(q): R[(f,) + which].forward()
    def finish(q, *which):
        for f, a, b in sets(q): R[(f,) + which].finish()

    e1 = Ring("E", "x", here, zero)
    qy = Ring("Q", "y", here, None)
    stage_one("a")
    to_sibling("E", here, (0, 0))
    weights = [pltpu.make_async_copy(a, b, wsem.at[i]) for i,(a,b) in enumerate(((wg_hbm,wg),(wu_hbm,wu),(wd_hbm,wd)))]
    e1.forward()
    forward("a", 1)
    stage_two("a", (-1, 1))
    e1.finish()
    def e_sib(step):
        at = moved(here, "z", step); at["x"] = None
        v = view("E", at)
        sibs["E", "col", step] = send(v, v, device("c", 0))
    col = dict(here); col["x"] = None
    e2 = Ring("E", "z", col, None)
    finish("a", 1)
    stage_two("a", (2,))
    qy.forward()
    e2.forward()
    e_sib(-1); e_sib(1)
    forward("a", 2, 0)
    qy.finish()
    stage_one("q")
    e2.finish()
    e_sib(2)
    for w in weights: w.start()
    for k in ((0, 0), (-1, 0), (1, 0), (2, 0)): sibs[("E",) + k].wait_recv()
    for s in (-1, 1, 2): sibs["E", "col", s].wait_recv()

    place = [((x + dx + 4) % 4, (z + dz + 4) % 4) for dx, dz in CHIPS]
    for n, (px, pz) in enumerate(place):
        for s in range(2):
            block = ex[px, pz, s].astype(F32)
            for q in range(3):
                rs[q, 2 * n + s:2 * n + s + 1, :] = block[q:q + 1]
    routes = [rs[0, :, k * 128:(k + 1) * 128] for k in range(8)]
    probs = [rs[1, :, k * 128:(k + 1) * 128] + rs[2, :, k * 128:(k + 1) * 128] for k in range(8)]
    tri = (lax.broadcasted_iota(jnp.int32, (128, 128), 0) < lax.broadcasted_iota(jnp.int32, (128, 128), 1)).astype(F32).astype(BF)
    for e in range(2):
        name = (dp * 2 + e).astype(F32)
        member = jnp.zeros((32, 128), F32); weight = jnp.zeros((32, 128), F32)
        for k in range(8):
            hit = routes[k] == name
            member = member + jnp.where(hit, 1.0, 0.0)
            weight = weight + jnp.where(hit, probs[k], 0.0)
        before = nn(member.astype(BF), tri)
        offset = ((lax.broadcasted_iota(jnp.int32, (32, 128), 0) % 4) * 20).astype(F32)
        target = jnp.where(member > 0.5, before + offset, -1.0)
        for g in range(8):
            t4 = jnp.concatenate([target[g * 4 + i:g * 4 + i + 1] for i in range(4)], axis=1)
            w4 = jnp.concatenate([weight[g * 4 + i:g * 4 + i + 1] for i in range(4)], axis=1)
            oh = jnp.where(lax.broadcasted_iota(jnp.int32, (80, 512), 0).astype(F32) == t4, 1.0, 0.0)
            onehot[g, e * 80:(e + 1) * 80, :] = oh.astype(BF)
            prob[e, g * 80:(g + 1) * 80, :] = jnp.broadcast_to(jnp.sum(oh * w4, axis=1, keepdims=True), (80, 128))

    waited = set()
    def need(q, g):
        for key in CHIPS[2 * g:2 * g + 2]:
            for f, a, b in sets(q):
                if (f, key) not in waited:
                    waited.add((f, key))
                    sibs[(f,) + key].wait_recv()
    base = pl.multiple_of(y * 1024, 1024)
    def pack_own(g):
        need("a", g)
        v = jnp.concatenate([ga[px, pz].reshape(256, CA) for px, pz in place[2 * g:2 * g + 2]], axis=0)
        out = nn(onehot[g], v).astype(BF)
        rows = pl.ds(g * 80, 80)
        for e in range(2):
            xh[e, rows, pl.ds(base, HA)] = out[e * 80:(e + 1) * 80, :HA]
            xg[e, rows, pl.ds(base, GA)] = out[e * 80:(e + 1) * 80, HA:]
    class Slots:
        def __init__(self, g):
            self.g = g
            self.up = [send(v, v, device("y", 1)) for v in self.refs(y)]
            self.down = [send(v, v, device("y", -1)) for v in self.refs(y)]
        def refs(self, yy, es=pl.ds(0, 2)):
            at = pl.multiple_of(yy * 1024, 1024)
            rows = pl.ds(self.g * 80, 80)
            return xh.at[es, rows, pl.ds(at, HA)], xg.at[es, rows, pl.ds(at, GA)]
        def forward(self):
            for w in self.up: w.wait_recv()
            self.up2 = [send(v, v, device("y", 1)) for v in self.refs((y + 3) % 4, pl.ds(0, 1))]
            for w in self.down: w.wait_recv()
            self.down2 = [send(v, v, device("y", -1)) for v in self.refs((y + 1) % 4, pl.ds(1, 1))]
        def finish(self):
            for w in self.up2 + self.down2: w.wait_recv()
            for w in self.up + self.down + self.up2 + self.down2:
                w.wait_send()
                pending[:] = [q for q in pending if q is not w]
    def q_copies(g, yy):
        return [pltpu.make_async_copy(gq.at[px, pz, :, yy], qb.at[yy, i], qsem.at[yy, i])
                for i, (px, pz) in enumerate(place[2 * g:2 * g + 2])]
    def q_start(g):
        for yy in range(4):
            for w in q_copies(g, yy): w.start()
    def pack_rest(groups):
        for g in groups: need("q", g)
        q_start(groups[0])
        for g, after in zip(groups, groups[1:] + (None,)):
            for yy in range(4):
                for w in q_copies(g, yy): w.wait()
                out = nn(onehot[g], qb[yy].reshape(512, CQ)).astype(BF)
                rows = pl.ds(g * 80, 80)
                for e in range(2):
                    xh[e, rows, yy * 1024 + HA:(yy + 1) * 1024] = out[e * 80:(e + 1) * 80, :1024 - HA]
                    xg[e, rows, yy * 1024 + GA:(yy + 1) * 1024] = out[e * 80:(e + 1) * 80, 1024 - HA:]
                if after is not None:
                    for w in q_copies(after, yy): w.start()
    def hidden_units(h, e):
        rows = pl.ds(h * 320, 320)
        gate[...] = jnp.zeros_like(gate); up[...] = jnp.zeros_like(up); back[...] = jnp.zeros_like(back)
        @pl.loop(0, 8)
        def _(kk):
            cols = pl.ds(pl.multiple_of(kk * 512, 512), 512)
            a = xh[e, rows, cols]
            gate[...] += nn(a, wg[e, cols, :])
            up[...] += nn(a, wu[e, cols, :])
            back[...] += nt(xg[e, rows, cols], wd[e, :, cols])
        @pl.loop(0, 4)
        def _(r):
            here_rows = pl.ds(pl.multiple_of(r * 80, 16), 80)
            all_rows = pl.ds(pl.multiple_of(h * 320 + r * 80, 16), 80)
            gp = gate[here_rows, :]; u = up[here_rows, :]; b = back[here_rows, :]
            sig = 1.0 / (1.0 + jnp.exp(-gp))
            act = gp * sig
            sprob[e, all_rows, :] = jnp.broadcast_to(jnp.sum(b * act * u, axis=1, keepdims=True), (80, 128))
            p = prob[e, all_rows, 0:1]
            gg[here_rows, :] = (b * u * sig * (1.0 + gp * (1.0 - sig)) * p).astype(BF)
            ug[here_rows, :] = (b * act * p).astype(BF)
        @pl.loop(0, 8)
        def _(kk):
            cols = pl.ds(pl.multiple_of(kk * 512, 512), 512)
            xh[e, rows, cols] = (nt(gg[...], wg[e, cols, :]) + nt(ug[...], wu[e, cols, :])).astype(BF)
        out_copies.append(pltpu.make_async_copy(xh.at[e, rows], ws_out.at[e, rows], wsem.at[3 + h * 2 + e]))
        out_copies[-1].start()

    out_copies = []
    oh_copy = pltpu.make_async_copy(onehot, oh_out, own_sem.at[0])
    oh_copy.start()
    S = {}
    forward("a", 2, -1)
    pack_own(0); S[0] = Slots(0)
    pack_own(1); S[1] = Slots(1)
    forward("a", 2, 1)
    pack_own(2); S[2] = Slots(2)
    pack_own(3)
    forward("a", 2, 2)
    for s in STEPS: finish("a", 2, s)
    for g in range(4, 8): pack_own(g)
    S[0].forward(); S[3] = Slots(3)
    S[1].forward(); S[4] = Slots(4)
    forward("q", 1)
    stage_two("q", (-1, 1))
    S[2].forward(); S[5] = Slots(5)
    forward("q", 2, 0)
    finish("q", 1)
    stage_two("q", (2,))
    S[3].forward(); S[6] = Slots(6)
    forward("q", 2, -1)
    pack_rest((0, 1))
    S[4].forward(); S[7] = Slots(7)
    forward("q", 2, 1)
    pack_rest((2, 3))
    for w in weights: w.wait()
    for g in range(4): S[g].finish()
    hidden_units(0, 0)
    S[5].forward()
    finish("q", 2, 0)
    forward("q", 2, 2)
    hidden_units(0, 1)
    S[6].forward()
    finish("q", 2, -1)
    finish("q", 2, 1)
    S[7].forward()
    finish("q", 2, 2)
    pack_rest((4, 5, 6, 7))
    for g in range(4, 8): S[g].finish()
    for e in range(2): hidden_units(1, e)

    for g in range(8):
        for e in range(2):
            oh = onehot[g, e * 80:(e + 1) * 80, :].astype(F32)
            row = jnp.sum(oh * sprob[e, g * 80:(g + 1) * 80, 0:1], axis=0, keepdims=True)
            for i in range(4):
                spt[e, g * 4 + i:g * 4 + i + 1, :] = row[:, i * 128:(i + 1) * 128]
    n0 = (dp * 2).astype(F32)
    line = lax.broadcasted_iota(jnp.int32, (32, 16, 128), 1)
    def routed(k):
        r = rs[0, :, k * 128:(k + 1) * 128]
        return (jnp.where(r == n0, spt[0], 0.0) + jnp.where(r == n0 + 1.0, spt[1], 0.0))[:, None, :]
    for k in range(4):
        rr[:, :, k * 128:(k + 1) * 128] = (jnp.where(line == 0, routed(k), 0.0) + jnp.where(line == 1, routed(k + 4), 0.0)).astype(BF)
    rr_copy = pltpu.make_async_copy(rr, rr_out, own_sem.at[1])
    rr_copy.start()
    oh_copy.wait()
    for w in out_copies: w.wait()
    rr_copy.wait()
    for s in pending: s.wait_send()

def experts(hid, gra, ext, wg, wu, wd):
    V=pltpu.VMEM
    A=pl.BlockSpec(memory_space=pl.ANY)
    N=4 + 3 + 7 + 4 + 2 * (40 + 32) + 64
    return pl.pallas_call(expert_kernel,
        out_shape=(jax.ShapeDtypeStruct((2,640,4096),BF), jax.ShapeDtypeStruct((8,160,512),BF), jax.ShapeDtypeStruct((32,16,512),BF), jax.ShapeDtypeStruct((4,4,2,4,128,CQ),BF)),
        in_specs=[A]*6, out_specs=(A,)*4,
        scratch_shapes=[V((2,4096,384),BF),V((2,4096,384),BF),V((2,384,4096),BF),
            V((2,640,4096),BF),V((2,640,4096),BF),V((4,4,2,128,CA),BF),V((4,4,2,16,1024),BF),V((3,32,1024),F32),V((32,16,512),BF),
            V((8,160,512),BF),V((2,640,128),F32),V((2,640,128),F32),V((4,2,2,128,CQ),BF),
            V((320,384),F32),V((320,384),F32),V((320,384),F32),V((320,384),BF),V((320,384),BF),V((2,32,128),F32),
            pltpu.SemaphoreType.DMA((5,)),pltpu.SemaphoreType.DMA((7,)),pltpu.SemaphoreType.DMA((4,2)),
            pltpu.SemaphoreType.DMA((N,)),pltpu.SemaphoreType.DMA((N,))],
        compiler_params=pltpu.CompilerParams(collective_id=0, has_side_effects=True, vmem_limit_bytes=63*1024*1024),
    )(hid, gra, ext, wg, wu, wd)[:3]

def return_kernel(ws_hbm, oh_hbm, rr_hbm, pick, grad, router, ws, onehot, rr, y1, y2, red, pq, sq, lq, pa, sa, la, ly, lr, fin, inc,
                  in_sem, g_sem, send_sem, recv_sem):
    dp = lax.axis_index("dp"); y = lax.axis_index("tensor")
    x = dp // 8; z = (dp // 2) % 4; c = dp % 2
    here = {"x": x, "y": y, "z": z}
    def device(axis, step):
        if axis == "c":
            return {"dp": x * 8 + z * 2 + (1 - c), "tensor": y}
        at = dict(here)
        at[axis] = (at[axis] + step + 4) % 4
        return {"dp": at["x"] * 8 + at["z"] * 2 + c, "tensor": at["y"]}
    mates = []
    for bit in range(3):
        low = (dp // (1 << bit)) % 2
        mates.append({"dp": dp + (1 - 2 * low) * (1 << bit), "tensor": y})
    def g_copy(g):
        rows = pl.ds(g * 80, 80)
        return pltpu.make_async_copy(ws_hbm.at[:, rows], ws.at[:, rows], g_sem.at[g])
    small = [pltpu.make_async_copy(oh_hbm, onehot, in_sem.at[0]), pltpu.make_async_copy(rr_hbm, rr, in_sem.at[1])]
    for s in small: s.start()
    for g in reversed(range(8)): g_copy(g).start()
    barrier = pltpu.get_barrier_semaphore()
    partners = [device(a, s) for a in "xyz" for s in (1, -1)] + [device("y", 2)] + mates
    for p in partners:
        pl.semaphore_signal(barrier, inc=1, device_id=p, device_id_type=MESH)
    pl.semaphore_wait(barrier, len(partners))

    number = [0]
    pending = []
    def send(src, dst, to):
        n = number[0]; number[0] += 1
        copy = pltpu.make_async_remote_copy(src_ref=src, dst_ref=dst, send_sem=send_sem.at[n],
            recv_sem=recv_sem.at[n], device_id=to, device_id_type=MESH)
        copy.start()
        pending.append(copy)
        return copy
    def add(dst, *terms):
        if len(dst.shape) == 3:
            @pl.loop(0, dst.shape[0])
            def _(i):
                total = terms[0][i].astype(F32)
                for t in terms[1:]: total = total + t[i].astype(F32)
                dst[i] = total.astype(BF)
        else:
            total = terms[0][...].astype(F32)
            for t in terms[1:]: total = total + t[...].astype(F32)
            dst[...] = total.astype(BF)
    class Ring:
        def __init__(self, axis, land, far_up, far_down):
            self.axis, self.land = axis, land
            self.up1 = send(far_up, land[0], device(axis, 1))
            self.down1 = send(far_down, land[1], device(axis, -1))
        def middle(self, after, after_up, before, before_down):
            self.up1.wait_recv()
            add(after_up, after_up, self.land[0])
            self.up2 = send(after, self.land[2], device(self.axis, 1))
            self.down1.wait_recv()
            add(before_down, before_down, self.land[1])
            self.down2 = send(before, self.land[3], device(self.axis, -1))
        def finish(self, near):
            self.up2.wait_recv(); self.down2.wait_recv()
            add(near, near, self.land[2], self.land[3])

    def slot(g, k, es=pl.ds(0, 2)):
        at = pl.multiple_of(((y + k + 4) % 4) * 1024, 1024)
        return ws.at[es, pl.ds(g * 80, 80), pl.ds(at, RA)]
    Y = {}
    def y_start(g):
        Y[g] = Ring("y", (y1.at[g, pl.ds(0, 1)], y1.at[g, pl.ds(1, 1)], y2.at[g, 0], y2.at[g, 1]),
                    slot(g, 2, pl.ds(0, 1)), slot(g, 2, pl.ds(1, 1)))
    def y_middle(g):
        Y[g].middle(slot(g, 1), slot(g, 1, pl.ds(0, 1)), slot(g, -1), slot(g, -1, pl.ds(1, 1)))
    def y_finish(g):
        Y[g].finish(slot(g, 0))
    def spread(g):
        return onehot[g].astype(F32).T.astype(BF)
    sib = {}
    def combine_rest(g):
        oht = spread(g)
        for t in range(4):
            v = jnp.concatenate([ws[e, g * 80:(g + 1) * 80, t * 1024 + RA:(t + 1) * 1024] for e in range(2)], axis=0)
            out = nn(oht, v).astype(BF)
            for i in range(4):
                pq[i % 2, 2 * g + i // 2, t] = out[i * 128:(i + 1) * 128]
        for n in (2 * g + 1, 2 * g):
            sib["q", n] = send(pq.at[1 - c, n], sq.at[n], device("c", 0))
    def combine_own(g):
        oht = spread(g)
        at = pl.ds(pl.multiple_of(y * 1024, 1024), RA)
        v = jnp.concatenate([ws[e, g * 80:(g + 1) * 80, at] for e in range(2)], axis=0)
        out = nn(oht, v).astype(BF)
        for i in range(4):
            pa[i % 2, 2 * g + i // 2, 16:144] = out[i * 128:(i + 1) * 128]
            pa[i % 2, 2 * g + i // 2, 0:16] = rr[g * 4 + i]
        for n in (2 * g + 1, 2 * g):
            sib["a", n] = send(pa.at[1 - c, n], sa.at[n], device("c", 0))
    def merge(q, n):
        sib[q, n].wait_recv()
        if q == "q":
            add(pq.at[c, n], pq.at[c, n], sq.at[n])
        else:
            add(pa.at[c, n], pa.at[c, n], sa.at[n])
    def block(q, f, n, part="all"):
        if q == "q":
            ts = {"all": pl.ds(0, 4), "up": pl.ds(0, 2), "down": pl.ds(2, 2)}[part]
            return pq.at[c, n, ts, pl.ds(64 * f, 64)]
        first, count = {"all": ((0, 80), (80, 64)), "up": ((0, 48), (80, 32)), "down": ((48, 32), (112, 32))}[part][f]
        return pa.at[c, n, pl.ds(first, count)]
    def land(q, f, r):
        if q == "q":
            v = lq.at[f, r]
            return v.at[pl.ds(0, 2)], v.at[pl.ds(2, 2)], v.at[pl.ds(4, 4)], v.at[pl.ds(8, 4)]
        up, down = ((48, 32), (32, 32))[f]
        v = la.at[f, r]
        return v.at[pl.ds(0, up)], v.at[pl.ds(48, down)], v.at[pl.ds(80, up + down)], v.at[pl.ds(160, up + down)]
    R = {}
    def chip(f, s, k):
        return CHIPS.index((s, k) if f == 0 else (k, s))
    def start_one(q, s):
        for f in (0, 1):
            n = chip(f, s, 2)
            R[q, f, s] = Ring("zx"[f], land(q, f, STEPS.index(s)), block(q, f, n, "up"), block(q, f, n, "down"))
    def middle_one(q, s):
        for f in (0, 1):
            a, b = chip(f, s, 1), chip(f, s, -1)
            R[q, f, s].middle(block(q, f, a), block(q, f, a, "up"), block(q, f, b), block(q, f, b, "down"))
    def finish_one(q, s):
        for f in (0, 1): R[q, f, s].finish(block(q, f, chip(f, s, 0)))
    def start_two(q):
        for f in (0, 1):
            n = chip(f, 2, 0)
            R[q, f, "two"] = Ring("xz"[f], land(q, f, 4), block(q, f, n, "up"), block(q, f, n, "down"))
    def middle_two(q):
        for f in (0, 1):
            a, b = chip(f, 1, 0), chip(f, -1, 0)
            R[q, f, "two"].middle(block(q, f, a), block(q, f, a, "up"), block(q, f, b), block(q, f, b, "down"))
    def finish_two(q):
        for f in (0, 1): R[q, f, "two"].finish(block(q, f, 0))

    for s in small: s.wait()
    for g in reversed(range(8)):
        g_copy(g).wait()
        y_start(g)
        combine_rest(g)
    for n in range(15, 8, -1): merge("q", n)
    for s in (2, 1, -1, 0): start_one("q", s)
    y_middle(7); y_middle(6)
    for n in range(8, 3, -1): merge("q", n)
    middle_one("q", 2)
    y_middle(5); y_middle(4)
    middle_one("q", 1)
    for n in range(3, -1, -1): merge("q", n)
    y_middle(3); y_middle(2)
    middle_one("q", -1)
    middle_one("q", 0)
    y_middle(1); y_middle(0)
    finish_one("q", 2)
    start_two("q")
    for g in (7, 6, 5, 4):
        y_finish(g); combine_own(g)
    finish_one("q", 1); finish_one("q", -1)
    middle_two("q")
    for g in (3, 2, 1, 0):
        y_finish(g); combine_own(g)
    for n in range(15, 8, -1): merge("a", n)
    for s in (2, 1, -1, 0): start_one("a", s)
    finish_one("q", 0)
    for n in range(8, -1, -1): merge("a", n)
    for s in (2, 1, -1, 0): middle_one("a", s)
    finish_two("q")
    def rest(k, part=pl.ds(0, 128)):
        return pq.at[c, 0, (y + k + 4) % 4, part]
    lo, hi = pl.ds(0, 64), pl.ds(64, 64)
    last = Ring("y", (ly.at[pl.ds(0, 64)], ly.at[pl.ds(64, 64)], ly.at[pl.ds(128, 128)], ly.at[pl.ds(256, 128)]), rest(2, lo), rest(2, hi))
    finish_one("a", 2)
    start_two("a")
    finish_one("a", 1); finish_one("a", -1)
    middle_two("a")
    last.middle(rest(1), rest(1, lo), rest(-1), rest(-1, hi))
    finish_one("a", 0)
    finish_two("a")
    odds = [send(pa.at[c, 0, pl.ds(0, 16)], lr.at[i], device("y", s)) for i, s in enumerate((1, 2, -1))]
    fin[:, 0:RA] = pa[c, 0, 16:144]
    last.finish(rest(0))
    fin[:, RA:1024] = pq[c, 0, y]
    swaps = [send(fin.at[64:128], inc.at[b], mates[b]) for b in range(3)]
    for o in odds: o.wait_recv()
    router[...] = (pa[c, 0, 0:16].astype(F32) + lr[0].astype(F32) + lr[1].astype(F32) + lr[2].astype(F32)).astype(BF)
    grad[0:64, :] = fin[0:64, :]
    for s in swaps: s.wait_recv()
    row = lax.broadcasted_iota(jnp.int32, (64, 1024), 0)
    kept = fin[64:128, :].astype(F32)
    taken = row >= 64 - pick[1]
    for b in range(3):
        kept = jnp.where(taken & (pick[0] == b), inc[b].astype(F32), kept)
    grad[64:128, :] = kept.astype(BF)
    for s in pending: s.wait_send()

def returned(ws, oh, rr, pick):
    V=pltpu.VMEM
    A=pl.BlockSpec(memory_space=pl.ANY)
    N=16 + 16 + 40 + 40 + 32 + 4 + 3 + 3
    return pl.pallas_call(return_kernel,
        out_shape=(jax.ShapeDtypeStruct((128,1024),BF),jax.ShapeDtypeStruct((16,RA),BF)),
        in_specs=[A,A,A,pl.BlockSpec(memory_space=pltpu.SMEM)],
        out_specs=(pl.BlockSpec(memory_space=V),pl.BlockSpec(memory_space=V)),
        scratch_shapes=[V((2,640,4096),BF),V((8,160,512),BF),V((32,16,RA),BF),
            V((8,2,80,RA),BF),V((8,2,2,80,RA),BF),V((8,128),F32),
            V((2,16,4,128,RQ),BF),V((16,4,128,RQ),BF),V((2,5,12,64,RQ),BF),
            V((2,16,144,RA),BF),V((16,144,RA),BF),V((2,5,240,RA),BF),
            V((384,RQ),BF),V((3,16,RA),BF),V((128,1024),BF),V((3,64,1024),BF),
            pltpu.SemaphoreType.DMA((2,)),pltpu.SemaphoreType.DMA((8,)),pltpu.SemaphoreType.DMA((N,)),pltpu.SemaphoreType.DMA((N,))],
        compiler_params=pltpu.CompilerParams(collective_id=1, has_side_effects=True, vmem_limit_bytes=63*1024*1024),
    )(ws, oh, rr, pick)

def local(hidden, grad_out, routes, route_probs, w_gate, w_up, w_down, partner, swap_count):
    flat = route_probs.T.reshape(1, 1024)
    high = lax.reduce_precision(flat, 8, 7).astype(BF)
    low = (flat - high.astype(F32)).astype(BF)
    number = routes.T.reshape(1, 1024).astype(BF)
    ext = jnp.concatenate([number, high, low, jnp.zeros((13, 1024), BF)], axis=0)
    ws, oh, rr = experts(hidden, grad_out, ext, w_gate, w_up, w_down)
    rank = lax.axis_index("dp")
    apart = jnp.bitwise_xor(partner[rank], rank)
    pick = jnp.stack([apart // 2, swap_count[rank]]).astype(jnp.int32)
    grad, router = returned(ws, oh, rr, pick)
    return grad, router[:2].reshape(8, 128).T


def solution(mesh):
    placed = (
        P("dp", "tensor"),
        P("dp", "tensor"),
        P("dp", None),
        P("dp", None),
        P("dp", None, "tensor"),
        P("dp", None, "tensor"),
        P("dp", "tensor", None),
        P(),
        P(),
    )
    return jax.shard_map(
        local,
        mesh=mesh,
        in_specs=placed,
        out_specs=(P("dp", "tensor"), P("dp", None)),
        check_vma=False,
    )
```

```python
import functools
import jax
import jax.numpy as jnp
from jax import lax
from jax.experimental import pallas as pl
from jax.experimental.pallas import tpu as pltpu
from jax.sharding import PartitionSpec as P

MESH = pl.DeviceIdType.MESH
BF=jnp.bfloat16; F32=jnp.float32
HA=640
GA=512
CA=HA+GA
CQ=2048-CA
STEPS=(0,-1,1,2)
CHIPS=((0,0),(0,-1),(-1,0),(-1,-1),(0,1),(1,0),(-1,1),(1,-1),(1,1),(0,2),(2,0),(-1,2),(2,-1),(1,2),(2,1),(2,2))
RA=512
RQ=1024-RA

def nt(a,b): return lax.dot_general(a,b,(((1,),(1,)),((),())),preferred_element_type=F32)
def nn(a,b): return jnp.dot(a,b,preferred_element_type=F32)

def expert_kernel(hid, gra, routes_ref, probs_ref, wg_hbm, wu_hbm, wd_hbm, ws_out, oh_out, rr_out, gq, wgu, wd, xh, xg, ga, qo, ex, rs, rr, onehot, prob, sprob, qb,
                  gu, back, ggu, spt, own_sem, wsem, qsem, send_sem, recv_sem):
    dp = lax.axis_index("dp"); y = lax.axis_index("tensor")
    x = dp // 8; z = (dp // 2) % 4; c = dp % 2
    here = {"x": x, "y": y, "z": z}
    def device(axis, step):
        if axis == "c":
            return {"dp": x * 8 + z * 2 + (1 - c), "tensor": y}
        at = dict(here)
        at[axis] = (at[axis] + step + 4) % 4
        return {"dp": at["x"] * 8 + at["z"] * 2 + c, "tensor": at["y"]}
    barrier = pltpu.get_barrier_semaphore()
    partners = [device(a, s) for a in "xyz" for s in (1, -1)] + [device("x", 2), device("z", 2), device("c", 0)]
    for p in partners:
        pl.semaphore_signal(barrier, inc=1, device_id=p, device_id_type=MESH)
    probs = probs_ref[...]
    high = probs.astype(BF).astype(F32)
    ex[x, z, c] = jnp.concatenate([routes_ref[...].astype(F32), high, probs - high, jnp.zeros((8, 128), F32)], axis=0).astype(BF)
    ga[x, z, c, :, 0:HA] = hid[:, 0:HA]
    ga[x, z, c, :, HA:CA] = gra[:, 0:GA]
    qo[:, 0:1024 - HA] = hid[:, HA:1024]
    qo[:, 1024 - HA:CQ] = gra[:, GA:1024]
    keep = pltpu.make_async_copy(qo, gq.at[x, z, c, y], own_sem.at[0])
    keep.start()
    pl.semaphore_wait(barrier, len(partners))

    number = [0]
    pending = []
    def send(src, dst, to):
        n = number[0]; number[0] += 1
        copy = pltpu.make_async_remote_copy(src_ref=src, dst_ref=dst, send_sem=send_sem.at[n],
            recv_sem=recv_sem.at[n], device_id=to, device_id_type=MESH)
        copy.start()
        pending.append(copy)
        return copy
    def view(fam, at, part="all"):
        xx = pl.ds(0, 4) if at["x"] is None else at["x"]
        if fam in ("alo", "ahi"):
            first = 0 if fam == "alo" else 64
            first, count = {"all": (first, 64), "up": (first, 32), "down": (first + 32, 32)}[part]
            return ga.at[xx, at["z"], c, pl.ds(first, count)]
        if fam in ("qlo", "qhi"):
            ys = {"all": pl.ds(0, 4), "up": pl.ds(0, 2), "down": pl.ds(2, 2)}[part]
            return gq.at[xx, at["z"], c, ys, pl.ds(0 if fam == "qlo" else 64, 64)]
        rows = {"all": (0, 128), "up": (0, 64), "down": (64, 64)}[part]
        return gq.at[x, z, c, at["y"], pl.ds(*rows)]
    sibs = {}
    def to_sibling(fam, at, key):
        if key is None: return
        v = view(fam, at)
        sibs[(fam,) + key] = send(v, v, device("c", 0))
    def moved(at, axis, step):
        q = dict(at); q[axis] = (here[axis] + step + 4) % 4
        return q
    class Ring:
        def __init__(self, fam, axis, at, off, src=None):
            self.fam, self.axis, self.at, self.off = fam, axis, at, off
            v = view(fam, at)
            self.up = send(v if src is None else src, v, device(axis, 1))
            self.down = send(v if src is None else src, v, device(axis, -1))
        def key(self, step):
            if self.off is None: return None
            o = dict(self.off); o[self.axis] = step
            return (o["x"], o["z"])
        def forward(self):
            f, a = self.fam, self.axis
            before, after = moved(self.at, a, -1), moved(self.at, a, 1)
            self.up.wait_recv()
            v = view(f, before, "up")
            self.up2 = send(v, v, device(a, 1))
            to_sibling(f, before, self.key(-1))
            self.down.wait_recv()
            v = view(f, after, "down")
            self.down2 = send(v, v, device(a, -1))
            to_sibling(f, after, self.key(1))
        def finish(self):
            self.up2.wait_recv()
            self.down2.wait_recv()
            to_sibling(self.fam, moved(self.at, self.axis, 2), self.key(2))
    def sets(q):
        return ((q + "lo", "x", "z"), (q + "hi", "z", "x"))
    R = {}
    zero = {"x": 0, "z": 0}
    def stage_one(q):
        for f, a, b in sets(q): R[f, 1] = Ring(f, a, here, zero)
        for f, a, b in sets(q): R[f, 2, 0] = Ring(f, b, here, zero)
        for f, a, b in sets(q): to_sibling(f, here, (0, 0))
    def stage_two(q, steps):
        for f, a, b in sets(q):
            for s in steps:
                off = dict(zero); off[a] = s
                R[f, 2, s] = Ring(f, b, moved(here, a, s), off)
    def forward(q, *which):
        for f, a, b in sets(q): R[(f,) + which].forward()
    def finish(q, *which):
        for f, a, b in sets(q): R[(f,) + which].finish()

    def table_sends(v, to):
        return [send(v, v, d) for d in to]
    e = table_sends(ex.at[x, z, c], [device("c", 0)])
    qy = Ring("Q", "y", here, None, qo)
    stage_one("a")
    weights = [pltpu.make_async_copy(a, b, wsem.at[i]) for i,(a,b) in enumerate(((wg_hbm, wgu.at[:, :, pl.ds(0, 384)]), (wu_hbm, wgu.at[:, :, pl.ds(384, 384)]), (wd_hbm, wd)))]
    for w in e: w.wait_recv()
    e = table_sends(ex.at[x, z], [device("x", s) for s in (1, 2, -1)])
    forward("a", 1)
    stage_two("a", (-1, 1))
    for w in e: w.wait_recv()
    e = table_sends(ex.at[:, z], [device("z", s) for s in (1, 2, -1)])
    qy.forward()
    finish("a", 1)
    stage_two("a", (2,))
    for w in e: w.wait_recv()
    for w in weights: w.start()

    place = [((x + dx + 4) % 4, (z + dz + 4) % 4) for dx, dz in CHIPS]
    for n, (px, pz) in enumerate(place):
        for s in range(2):
            block = ex[px, pz, s].astype(F32)
            for q in range(24):
                rs[q, 2 * n + s:2 * n + s + 1, :] = block[q:q + 1]
    routes = [rs[k] for k in range(8)]
    probs = [rs[8 + k] + rs[16 + k] for k in range(8)]
    tri = (lax.broadcasted_iota(jnp.int32, (128, 128), 0) < lax.broadcasted_iota(jnp.int32, (128, 128), 1)).astype(F32).astype(BF)
    for e in range(2):
        name = (dp * 2 + e).astype(F32)
        member = jnp.zeros((32, 128), F32); weight = jnp.zeros((32, 128), F32)
        for k in range(8):
            hit = routes[k] == name
            member = member + jnp.where(hit, 1.0, 0.0)
            weight = weight + jnp.where(hit, probs[k], 0.0)
        before = nn(member.astype(BF), tri)
        offset = ((lax.broadcasted_iota(jnp.int32, (32, 128), 0) % 4) * 20).astype(F32)
        target = jnp.where(member > 0.5, before + offset, -1.0)
        for g in range(8):
            t4 = jnp.concatenate([target[g * 4 + i:g * 4 + i + 1] for i in range(4)], axis=1)
            w4 = jnp.concatenate([weight[g * 4 + i:g * 4 + i + 1] for i in range(4)], axis=1)
            oh = jnp.where(lax.broadcasted_iota(jnp.int32, (80, 512), 0).astype(F32) == t4, 1.0, 0.0)
            onehot[g, e * 80:(e + 1) * 80, :] = oh.astype(BF)
            prob[e, g * 80:(g + 1) * 80, :] = jnp.broadcast_to(jnp.sum(oh * w4, axis=1, keepdims=True), (80, 128))

    forward("a", 2, 0)
    qy.finish()
    keep.wait()
    stage_one("q")
    waited = set()
    def need(q, g):
        for key in CHIPS[2 * g:2 * g + 2]:
            for f, a, b in sets(q):
                if (f, key) not in waited:
                    waited.add((f, key))
                    sibs[(f,) + key].wait_recv()
    base = pl.multiple_of(y * 1024, 1024)
    def pack_own(g):
        need("a", g)
        v = jnp.concatenate([ga[px, pz].reshape(256, CA) for px, pz in place[2 * g:2 * g + 2]], axis=0)
        out = nn(onehot[g], v).astype(BF)
        rows = pl.ds(g * 80, 80)
        for e in range(2):
            xh[e, rows, pl.ds(base, HA)] = out[e * 80:(e + 1) * 80, :HA]
            xg[e, rows, pl.ds(base, GA)] = out[e * 80:(e + 1) * 80, HA:]
    class Slots:
        def __init__(self, g):
            self.g = g
            self.up = [send(v, v, device("y", 1)) for v in self.refs(y)]
            self.down = [send(v, v, device("y", -1)) for v in self.refs(y)]
        def refs(self, yy, es=pl.ds(0, 2)):
            at = pl.multiple_of(yy * 1024, 1024)
            rows = pl.ds(self.g * 80, 80)
            return xh.at[es, rows, pl.ds(at, HA)], xg.at[es, rows, pl.ds(at, GA)]
        def forward(self):
            for w in self.up: w.wait_recv()
            self.up2 = [send(v, v, device("y", 1)) for v in self.refs((y + 3) % 4, pl.ds(0, 1))]
            for w in self.down: w.wait_recv()
            self.down2 = [send(v, v, device("y", -1)) for v in self.refs((y + 1) % 4, pl.ds(1, 1))]
        def finish(self):
            for w in self.up2 + self.down2: w.wait_recv()
            for w in self.up + self.down + self.up2 + self.down2:
                w.wait_send()
                pending[:] = [q for q in pending if q is not w]
    def q_copies(g, yy):
        return [pltpu.make_async_copy(gq.at[px, pz, :, yy], qb.at[yy, i], qsem.at[yy, i])
                for i, (px, pz) in enumerate(place[2 * g:2 * g + 2])]
    def q_start(g):
        for yy in range(4):
            for w in q_copies(g, yy): w.start()
    def pack_rest(groups):
        for g in groups: need("q", g)
        q_start(groups[0])
        for g, after in zip(groups, groups[1:] + (None,)):
            for yy in range(4):
                for w in q_copies(g, yy): w.wait()
                out = nn(onehot[g], qb[yy].reshape(512, CQ)).astype(BF)
                rows = pl.ds(g * 80, 80)
                for e in range(2):
                    xh[e, rows, yy * 1024 + HA:(yy + 1) * 1024] = out[e * 80:(e + 1) * 80, :1024 - HA]
                    xg[e, rows, yy * 1024 + GA:(yy + 1) * 1024] = out[e * 80:(e + 1) * 80, 1024 - HA:]
                if after is not None:
                    for w in q_copies(after, yy): w.start()
    spans = ((0, 400), (400, 240))
    def units_in(h, e):
        first, count = spans[h]
        rows = pl.ds(first, count)
        part = pl.ds(0, count)
        @pl.loop(0, 4)
        def _(kk):
            cols = pl.ds(pl.multiple_of(kk * 1024, 1024), 1024)
            both = nn(xh[e, rows, cols], wgu[e, cols, :])
            last = nt(xg[e, rows, cols], wd[e, :, cols])
            @pl.when(kk == 0)
            def _():
                gu[part] = both
                back[part] = last
            @pl.when(kk > 0)
            def _():
                gu[part] += both
                back[part] += last
    def units_out(h, e):
        first, count = spans[h]
        rows = pl.ds(first, count)
        @pl.loop(0, count // 80)
        def _(r):
            here_rows = pl.ds(pl.multiple_of(r * 80, 16), 80)
            all_rows = pl.ds(pl.multiple_of(first + r * 80, 16), 80)
            gp = gu[here_rows, 0:384]; u = gu[here_rows, 384:768]; b = back[here_rows, :]
            sig = 1.0 / (1.0 + jnp.exp(-gp))
            act = gp * sig
            sprob[e, all_rows, :] = jnp.broadcast_to(jnp.sum(b * act * u, axis=1, keepdims=True), (80, 128))
            p = prob[e, all_rows, 0:1]
            ggu[here_rows, 0:384] = (b * u * sig * (1.0 + gp * (1.0 - sig)) * p).astype(BF)
            ggu[here_rows, 384:768] = (b * act * p).astype(BF)
        @pl.loop(0, 4)
        def _(kk):
            cols = pl.ds(pl.multiple_of(kk * 1024, 1024), 1024)
            xh[e, rows, cols] = nt(ggu[0:count], wgu[e, cols, :]).astype(BF)
        out_copies.append(pltpu.make_async_copy(xh.at[e, rows], ws_out.at[e, rows], wsem.at[3 + h * 2 + e]))
        out_copies[-1].start()

    out_copies = []
    oh_copy = pltpu.make_async_copy(onehot, oh_out, own_sem.at[2])
    oh_copy.start()
    S = {}
    forward("a", 2, -1)
    pack_own(0); S[0] = Slots(0)
    pack_own(1); S[1] = Slots(1)
    forward("a", 2, 1)
    pack_own(2); S[2] = Slots(2)
    pack_own(3)
    forward("a", 2, 2)
    for s in STEPS: finish("a", 2, s)
    for g in range(4, 8): pack_own(g)
    S[0].forward(); S[3] = Slots(3)
    S[1].forward(); S[4] = Slots(4)
    forward("q", 1)
    stage_two("q", (-1, 1))
    S[2].forward(); S[5] = Slots(5)
    forward("q", 2, 0)
    finish("q", 1)
    stage_two("q", (2,))
    S[3].forward(); S[6] = Slots(6)
    forward("q", 2, -1)
    pack_rest((0, 1))
    S[4].forward(); S[7] = Slots(7)
    forward("q", 2, 1)
    pack_rest((2, 3))
    finish("q", 2, 0)
    pack_rest((4,))
    for w in weights: w.wait()
    for g in range(5): S[g].finish()
    units_in(0, 0)
    S[5].forward()
    finish("q", 2, -1)
    units_out(0, 0)
    forward("q", 2, 2)
    S[6].forward()
    units_in(0, 1)
    finish("q", 2, 1)
    S[7].forward()
    units_out(0, 1)
    finish("q", 2, 2)
    pack_rest((5, 6, 7))
    for g in range(5, 8): S[g].finish()
    for e in range(2):
        units_in(1, e)
        units_out(1, e)

    for g in range(8):
        for e in range(2):
            oh = onehot[g, e * 80:(e + 1) * 80, :].astype(F32)
            row = jnp.sum(oh * sprob[e, g * 80:(g + 1) * 80, 0:1], axis=0, keepdims=True)
            for i in range(4):
                spt[e, g * 4 + i:g * 4 + i + 1, :] = row[:, i * 128:(i + 1) * 128]
    n0 = (dp * 2).astype(F32)
    line = lax.broadcasted_iota(jnp.int32, (32, 16, 128), 1)
    def routed(k):
        r = rs[k]
        return (jnp.where(r == n0, spt[0], 0.0) + jnp.where(r == n0 + 1.0, spt[1], 0.0))[:, None, :]
    for k in range(4):
        rr[:, :, k * 128:(k + 1) * 128] = (jnp.where(line == 0, routed(k), 0.0) + jnp.where(line == 1, routed(k + 4), 0.0)).astype(BF)
    rr_copy = pltpu.make_async_copy(rr, rr_out, own_sem.at[1])
    rr_copy.start()
    oh_copy.wait()
    for w in out_copies: w.wait()
    rr_copy.wait()
    for s in pending: s.wait_send()

def experts(hid, gra, routes, probs, wg, wu, wd):
    V=pltpu.VMEM
    A=pl.BlockSpec(memory_space=pl.ANY)
    N=7 + 4 + 2 * (40 + 32) + 64
    return pl.pallas_call(expert_kernel,
        out_shape=(jax.ShapeDtypeStruct((2,640,4096),BF), jax.ShapeDtypeStruct((8,160,512),BF), jax.ShapeDtypeStruct((32,16,512),BF), jax.ShapeDtypeStruct((4,4,2,4,128,CQ),BF)),
        in_specs=[pl.BlockSpec(memory_space=V)]*4+[A]*3, out_specs=(A,)*4,
        scratch_shapes=[V((2,4096,768),BF),V((2,384,4096),BF),
            V((2,640,4096),BF),V((2,640,4096),BF),V((4,4,2,128,CA),BF),V((128,CQ),BF),V((4,4,2,32,128),BF),V((24,32,128),F32),V((32,16,512),BF),
            V((8,160,512),BF),V((2,640,128),F32),V((2,640,128),F32),V((4,2,2,128,CQ),BF),
            V((400,768),F32),V((400,384),F32),V((400,768),BF),V((2,32,128),F32),
            pltpu.SemaphoreType.DMA((5,)),pltpu.SemaphoreType.DMA((7,)),pltpu.SemaphoreType.DMA((4,2)),
            pltpu.SemaphoreType.DMA((N,)),pltpu.SemaphoreType.DMA((N,))],
        compiler_params=pltpu.CompilerParams(collective_id=0, has_side_effects=True, vmem_limit_bytes=63*1024*1024),
    )(hid, gra, routes, probs, wg, wu, wd)[:3]

def return_kernel(ws_hbm, oh_hbm, rr_hbm, partner, swap_count, grad, router, ws, onehot, rr, y1, y2, red, pq, sq, lq, pa, sa, la, ly, lr, fin, inc,
                  in_sem, g_sem, send_sem, recv_sem):
    dp = lax.axis_index("dp"); y = lax.axis_index("tensor")
    x = dp // 8; z = (dp // 2) % 4; c = dp % 2
    here = {"x": x, "y": y, "z": z}
    def device(axis, step):
        if axis == "c":
            return {"dp": x * 8 + z * 2 + (1 - c), "tensor": y}
        at = dict(here)
        at[axis] = (at[axis] + step + 4) % 4
        return {"dp": at["x"] * 8 + at["z"] * 2 + c, "tensor": at["y"]}
    mates = []
    for bit in range(3):
        low = (dp // (1 << bit)) % 2
        mates.append({"dp": dp + (1 - 2 * low) * (1 << bit), "tensor": y})
    def g_copy(g):
        rows = pl.ds(g * 80, 80)
        return pltpu.make_async_copy(ws_hbm.at[:, rows], ws.at[:, rows], g_sem.at[g])
    small = [pltpu.make_async_copy(oh_hbm, onehot, in_sem.at[0]), pltpu.make_async_copy(rr_hbm, rr, in_sem.at[1])]
    for s in small: s.start()
    for g in reversed(range(8)): g_copy(g).start()
    barrier = pltpu.get_barrier_semaphore()
    partners = [device(a, s) for a in "xyz" for s in (1, -1)] + [device("y", 2)] + mates
    for p in partners:
        pl.semaphore_signal(barrier, inc=1, device_id=p, device_id_type=MESH)
    pl.semaphore_wait(barrier, len(partners))

    number = [0]
    pending = []
    def send(src, dst, to):
        n = number[0]; number[0] += 1
        copy = pltpu.make_async_remote_copy(src_ref=src, dst_ref=dst, send_sem=send_sem.at[n],
            recv_sem=recv_sem.at[n], device_id=to, device_id_type=MESH)
        copy.start()
        pending.append(copy)
        return copy
    def add(dst, *terms):
        if len(dst.shape) == 3:
            @pl.loop(0, dst.shape[0])
            def _(i):
                total = terms[0][i].astype(F32)
                for t in terms[1:]: total = total + t[i].astype(F32)
                dst[i] = total.astype(BF)
        else:
            total = terms[0][...].astype(F32)
            for t in terms[1:]: total = total + t[...].astype(F32)
            dst[...] = total.astype(BF)
    class Ring:
        def __init__(self, axis, land, far_up, far_down):
            self.axis, self.land = axis, land
            self.up1 = send(far_up, land[0], device(axis, 1))
            self.down1 = send(far_down, land[1], device(axis, -1))
        def middle(self, after, after_up, before, before_down):
            self.up1.wait_recv()
            add(after_up, after_up, self.land[0])
            self.up2 = send(after, self.land[2], device(self.axis, 1))
            self.down1.wait_recv()
            add(before_down, before_down, self.land[1])
            self.down2 = send(before, self.land[3], device(self.axis, -1))
        def finish(self, near):
            self.up2.wait_recv(); self.down2.wait_recv()
            add(near, near, self.land[2], self.land[3])

    def slot(g, k, es=pl.ds(0, 2)):
        at = pl.multiple_of(((y + k + 4) % 4) * 1024, 1024)
        return ws.at[es, pl.ds(g * 80, 80), pl.ds(at, RA)]
    Y = {}
    def y_start(g):
        Y[g] = Ring("y", (y1.at[g, pl.ds(0, 1)], y1.at[g, pl.ds(1, 1)], y2.at[g, 0], y2.at[g, 1]),
                    slot(g, 2, pl.ds(0, 1)), slot(g, 2, pl.ds(1, 1)))
    def y_middle(g):
        Y[g].middle(slot(g, 1), slot(g, 1, pl.ds(0, 1)), slot(g, -1), slot(g, -1, pl.ds(1, 1)))
    def y_finish(g):
        Y[g].finish(slot(g, 0))
    def spread(g):
        return onehot[g].astype(F32).T.astype(BF)
    sib = {}
    def combine_rest(g):
        oht = spread(g)
        for t in range(4):
            v = jnp.concatenate([ws[e, g * 80:(g + 1) * 80, t * 1024 + RA:(t + 1) * 1024] for e in range(2)], axis=0)
            out = nn(oht, v).astype(BF)
            for i in range(4):
                pq[i % 2, 2 * g + i // 2, t] = out[i * 128:(i + 1) * 128]
        for n in (2 * g + 1, 2 * g):
            sib["q", n] = send(pq.at[1 - c, n], sq.at[n], device("c", 0))
    def combine_own(g):
        oht = spread(g)
        at = pl.ds(pl.multiple_of(y * 1024, 1024), RA)
        v = jnp.concatenate([ws[e, g * 80:(g + 1) * 80, at] for e in range(2)], axis=0)
        out = nn(oht, v).astype(BF)
        for i in range(4):
            pa[i % 2, 2 * g + i // 2, 16:144] = out[i * 128:(i + 1) * 128]
            pa[i % 2, 2 * g + i // 2, 0:16] = rr[g * 4 + i]
        for n in (2 * g + 1, 2 * g):
            sib["a", n] = send(pa.at[1 - c, n], sa.at[n], device("c", 0))
    def merge(q, n):
        sib[q, n].wait_recv()
        if q == "q":
            add(pq.at[c, n], pq.at[c, n], sq.at[n])
        else:
            add(pa.at[c, n], pa.at[c, n], sa.at[n])
    def block(q, f, n, part="all"):
        if q == "q":
            ts = {"all": pl.ds(0, 4), "up": pl.ds(0, 2), "down": pl.ds(2, 2)}[part]
            return pq.at[c, n, ts, pl.ds(64 * f, 64)]
        first, count = {"all": ((0, 80), (80, 64)), "up": ((0, 48), (80, 32)), "down": ((48, 32), (112, 32))}[part][f]
        return pa.at[c, n, pl.ds(first, count)]
    def land(q, f, r):
        if q == "q":
            v = lq.at[f, r]
            return v.at[pl.ds(0, 2)], v.at[pl.ds(2, 2)], v.at[pl.ds(4, 4)], v.at[pl.ds(8, 4)]
        up, down = ((48, 32), (32, 32))[f]
        v = la.at[f, r]
        return v.at[pl.ds(0, up)], v.at[pl.ds(48, down)], v.at[pl.ds(80, up + down)], v.at[pl.ds(160, up + down)]
    R = {}
    def chip(f, s, k):
        return CHIPS.index((s, k) if f == 0 else (k, s))
    def start_one(q, s):
        for f in (0, 1):
            n = chip(f, s, 2)
            R[q, f, s] = Ring("zx"[f], land(q, f, STEPS.index(s)), block(q, f, n, "up"), block(q, f, n, "down"))
    def middle_one(q, s):
        for f in (0, 1):
            a, b = chip(f, s, 1), chip(f, s, -1)
            R[q, f, s].middle(block(q, f, a), block(q, f, a, "up"), block(q, f, b), block(q, f, b, "down"))
    def finish_one(q, s):
        for f in (0, 1): R[q, f, s].finish(block(q, f, chip(f, s, 0)))
    def start_two(q):
        for f in (0, 1):
            n = chip(f, 2, 0)
            R[q, f, "two"] = Ring("xz"[f], land(q, f, 4), block(q, f, n, "up"), block(q, f, n, "down"))
    def middle_two(q):
        for f in (0, 1):
            a, b = chip(f, 1, 0), chip(f, -1, 0)
            R[q, f, "two"].middle(block(q, f, a), block(q, f, a, "up"), block(q, f, b), block(q, f, b, "down"))
    def finish_two(q):
        for f in (0, 1): R[q, f, "two"].finish(block(q, f, 0))

    for s in small: s.wait()
    def group(g):
        g_copy(g).wait()
        y_start(g)
        combine_rest(g)
    def own(*gs):
        for g in gs:
            y_finish(g); combine_own(g)
    def merges(q, *ns):
        for n in ns: merge(q, n)
    group(7); group(6)
    merges("q", 15); start_one("q", 2)
    group(5)
    merges("q", 14, 13); start_one("q", 1)
    group(4)
    merges("q", 12, 11); start_one("q", -1)
    y_middle(7); group(3)
    merges("q", 10, 9); start_one("q", 0)
    y_middle(6); group(2)
    merges("q", 8); middle_one("q", 2)
    y_middle(5); group(1)
    merges("q", 7, 6); middle_one("q", 1)
    y_middle(4); group(0)
    merges("q", 5, 4, 3); middle_one("q", -1)
    own(7, 6)
    y_middle(3)
    merges("q", 2, 1, 0); middle_one("q", 0)
    y_middle(2)
    own(5, 4)
    finish_one("q", 2); start_two("q")
    merges("a", 15, 14, 13, 12, 11, 10, 9)
    for s in (2, 1, -1, 0): start_one("a", s)
    y_middle(1); y_middle(0)
    finish_one("q", 1); finish_one("q", -1); middle_two("q")
    merges("a", 8); middle_one("a", 2)
    own(3, 2, 1, 0)
    finish_one("q", 0)
    merges("a", 7, 6); middle_one("a", 1)
    merges("a", 5, 4, 3); middle_one("a", -1)
    merges("a", 2, 1, 0); middle_one("a", 0)
    finish_one("a", 2); start_two("a")
    finish_two("q")
    def rest(k, part=pl.ds(0, 128)):
        return pq.at[c, 0, (y + k + 4) % 4, part]
    lo, hi = pl.ds(0, 64), pl.ds(64, 64)
    last = Ring("y", (ly.at[pl.ds(0, 64)], ly.at[pl.ds(64, 64)], ly.at[pl.ds(128, 128)], ly.at[pl.ds(256, 128)]), rest(2, lo), rest(2, hi))
    finish_one("a", 1); finish_one("a", -1)
    middle_two("a")
    last.middle(rest(1), rest(1, lo), rest(-1), rest(-1, hi))
    finish_one("a", 0)
    finish_two("a")
    odds = [send(pa.at[c, 0, pl.ds(0, 16)], lr.at[i], device("y", s)) for i, s in enumerate((1, 2, -1))]
    fin[:, 0:RA] = pa[c, 0, 16:144]
    last.finish(rest(0))
    fin[:, RA:1024] = pq[c, 0, y]
    swaps = [send(fin.at[64:128], inc.at[b], mates[b]) for b in range(3)]
    for o in odds: o.wait_recv()
    total = pa[c, 0, 0:16].astype(F32) + lr[0].astype(F32) + lr[1].astype(F32) + lr[2].astype(F32)
    table = jnp.concatenate([total[k // 4:k // 4 + 1, (k % 4) * 128:(k % 4 + 1) * 128] for k in range(8)], axis=0)
    router[...] = table.astype(BF)
    grad[0:64, :] = fin[0:64, :]
    for s in swaps: s.wait_recv()
    row = lax.broadcasted_iota(jnp.int32, (64, 1024), 0)
    kept = fin[64:128, :].astype(F32)
    taken = row >= 64 - swap_count[dp]
    apart = jnp.bitwise_xor(partner[dp], dp)
    for b in range(3):
        kept = jnp.where(taken & (apart == (1 << b)), inc[b].astype(F32), kept)
    grad[64:128, :] = kept.astype(BF)
    for s in pending: s.wait_send()

def returned(ws, oh, rr, partner, swap_count):
    V=pltpu.VMEM
    A=pl.BlockSpec(memory_space=pl.ANY)
    N=16 + 16 + 40 + 40 + 32 + 4 + 3 + 3
    return pl.pallas_call(return_kernel,
        out_shape=(jax.ShapeDtypeStruct((128,1024),BF),jax.ShapeDtypeStruct((8,128),BF)),
        in_specs=[A,A,A,pl.BlockSpec(memory_space=pltpu.SMEM),pl.BlockSpec(memory_space=pltpu.SMEM)],
        out_specs=(pl.BlockSpec(memory_space=V),pl.BlockSpec(memory_space=V)),
        scratch_shapes=[V((2,640,4096),BF),V((8,160,512),BF),V((32,16,RA),BF),
            V((8,2,80,RA),BF),V((8,2,2,80,RA),BF),V((8,128),F32),
            V((2,16,4,128,RQ),BF),V((16,4,128,RQ),BF),V((2,5,12,64,RQ),BF),
            V((2,16,144,RA),BF),V((16,144,RA),BF),V((2,5,240,RA),BF),
            V((384,RQ),BF),V((3,16,RA),BF),V((128,1024),BF),V((3,64,1024),BF),
            pltpu.SemaphoreType.DMA((2,)),pltpu.SemaphoreType.DMA((8,)),pltpu.SemaphoreType.DMA((N,)),pltpu.SemaphoreType.DMA((N,))],
        compiler_params=pltpu.CompilerParams(collective_id=1, has_side_effects=True, vmem_limit_bytes=63*1024*1024),
    )(ws, oh, rr, partner, swap_count)

def local(hidden, grad_out, routes, route_probs, w_gate, w_up, w_down, partner, swap_count):
    ws, oh, rr = experts(hidden, grad_out, routes.T, route_probs.T, w_gate, w_up, w_down)
    grad, router = returned(ws, oh, rr, partner, swap_count)
    return grad, router.T


def solution(mesh):
    placed = (
        P("dp", "tensor"),
        P("dp", "tensor"),
        P("dp", None),
        P("dp", None),
        P("dp", None, "tensor"),
        P("dp", None, "tensor"),
        P("dp", "tensor", None),
        P(),
        P(),
    )
    return jax.shard_map(
        local,
        mesh=mesh,
        in_specs=placed,
        out_specs=(P("dp", "tensor"), P("dp", None)),
        check_vma=False,
    )
```

```python
import functools
import jax
import jax.numpy as jnp
from jax import lax
from jax.experimental import pallas as pl
from jax.experimental.pallas import tpu as pltpu
from jax.sharding import PartitionSpec as P

MESH = pl.DeviceIdType.MESH
BF=jnp.bfloat16; F32=jnp.float32
HA=512
GA=512
CA=HA+GA
CQ=2048-CA
STEPS=(0,-1,1,2)
CHIPS=((0,0),(0,-1),(-1,0),(-1,-1),(0,1),(1,0),(-1,1),(1,-1),(1,1),(0,2),(2,0),(-1,2),(2,-1),(1,2),(2,1),(2,2))
RA=512
RQ=1024-RA

def nt(a,b): return lax.dot_general(a,b,(((1,),(1,)),((),())),preferred_element_type=F32)
def nn(a,b): return jnp.dot(a,b,preferred_element_type=F32)

def expert_kernel(hid, gra, routes_ref, probs_ref, wg_hbm, wu_hbm, wd_hbm, ws_out, oh_out, rr_out, gq, wgu, wd, xh, xg, ga, qo, ex, rs, rr, onehot, prob, sprob, qb,
                  gu, back, ggu, spt, own_sem, wsem, qsem, send_sem, recv_sem):
    dp = lax.axis_index("dp"); y = lax.axis_index("tensor")
    x = dp // 8; z = (dp // 2) % 4; c = dp % 2
    here = {"x": x, "y": y, "z": z}
    def device(axis, step):
        if axis == "c":
            return {"dp": x * 8 + z * 2 + (1 - c), "tensor": y}
        at = dict(here)
        at[axis] = (at[axis] + step + 4) % 4
        return {"dp": at["x"] * 8 + at["z"] * 2 + c, "tensor": at["y"]}
    barrier = pltpu.get_barrier_semaphore()
    partners = [device(a, s) for a in "xyz" for s in (1, -1)] + [device("x", 2), device("z", 2), device("c", 0)]
    for p in partners:
        pl.semaphore_signal(barrier, inc=1, device_id=p, device_id_type=MESH)
    probs = probs_ref[...]
    high = probs.astype(BF).astype(F32)
    ex[x, z, c] = jnp.concatenate([routes_ref[...].astype(F32), high, probs - high, jnp.zeros((8, 128), F32)], axis=0).astype(BF)
    ga[x, z, c, :, 0:HA] = hid[:, 0:HA]
    ga[x, z, c, :, HA:CA] = gra[:, 0:GA]
    qo[:, 0:1024 - HA] = hid[:, HA:1024]
    qo[:, 1024 - HA:CQ] = gra[:, GA:1024]
    keep = pltpu.make_async_copy(qo, gq.at[x, z, c, y], own_sem.at[0])
    keep.start()
    pl.semaphore_wait(barrier, len(partners))

    number = [0]
    pending = []
    def send(src, dst, to):
        n = number[0]; number[0] += 1
        copy = pltpu.make_async_remote_copy(src_ref=src, dst_ref=dst, send_sem=send_sem.at[n],
            recv_sem=recv_sem.at[n], device_id=to, device_id_type=MESH)
        copy.start()
        pending.append(copy)
        return copy
    def view(fam, at, part="all"):
        xx = pl.ds(0, 4) if at["x"] is None else at["x"]
        if fam in ("alo", "ahi"):
            first = 0 if fam == "alo" else 64
            first, count = {"all": (first, 64), "up": (first, 32), "down": (first + 32, 32)}[part]
            return ga.at[xx, at["z"], c, pl.ds(first, count)]
        if fam in ("qlo", "qhi"):
            ys = {"all": pl.ds(0, 4), "up": pl.ds(0, 2), "down": pl.ds(2, 2)}[part]
            return gq.at[xx, at["z"], c, ys, pl.ds(0 if fam == "qlo" else 64, 64)]
        rows = {"all": (0, 128), "up": (0, 64), "down": (64, 64)}[part]
        return gq.at[x, z, c, at["y"], pl.ds(*rows)]
    sibs = {}
    def to_sibling(fam, at, key):
        if key is None: return
        v = view(fam, at)
        sibs[(fam,) + key] = send(v, v, device("c", 0))
    def moved(at, axis, step):
        q = dict(at); q[axis] = (here[axis] + step + 4) % 4
        return q
    class Ring:
        def __init__(self, fam, axis, at, off, src=None):
            self.fam, self.axis, self.at, self.off = fam, axis, at, off
            v = view(fam, at)
            self.up = send(v if src is None else src, v, device(axis, 1))
            self.down = send(v if src is None else src, v, device(axis, -1))
        def key(self, step):
            if self.off is None: return None
            o = dict(self.off); o[self.axis] = step
            return (o["x"], o["z"])
        def forward(self):
            f, a = self.fam, self.axis
            before, after = moved(self.at, a, -1), moved(self.at, a, 1)
            self.up.wait_recv()
            v = view(f, before, "up")
            self.up2 = send(v, v, device(a, 1))
            to_sibling(f, before, self.key(-1))
            self.down.wait_recv()
            v = view(f, after, "down")
            self.down2 = send(v, v, device(a, -1))
            to_sibling(f, after, self.key(1))
        def finish(self):
            self.up2.wait_recv()
            self.down2.wait_recv()
            to_sibling(self.fam, moved(self.at, self.axis, 2), self.key(2))
    def sets(q):
        return ((q + "lo", "x", "z"), (q + "hi", "z", "x"))
    R = {}
    zero = {"x": 0, "z": 0}
    def stage_one(q):
        for f, a, b in sets(q): R[f, 1] = Ring(f, a, here, zero)
        for f, a, b in sets(q): R[f, 2, 0] = Ring(f, b, here, zero)
        for f, a, b in sets(q): to_sibling(f, here, (0, 0))
    def stage_two(q, steps):
        for f, a, b in sets(q):
            for s in steps:
                off = dict(zero); off[a] = s
                R[f, 2, s] = Ring(f, b, moved(here, a, s), off)
    def forward(q, *which):
        for f, a, b in sets(q): R[(f,) + which].forward()
    def finish(q, *which):
        for f, a, b in sets(q): R[(f,) + which].finish()

    def table_sends(v, to):
        return [send(v, v, d) for d in to]
    e = table_sends(ex.at[x, z, c], [device("c", 0)])
    qy = Ring("Q", "y", here, None, qo)
    stage_one("a")
    weights = [pltpu.make_async_copy(a, b, wsem.at[i]) for i,(a,b) in enumerate(((wg_hbm, wgu.at[:, :, pl.ds(0, 384)]), (wu_hbm, wgu.at[:, :, pl.ds(384, 384)]), (wd_hbm, wd)))]
    for w in e: w.wait_recv()
    e = table_sends(ex.at[x, z], [device("x", s) for s in (1, 2, -1)])
    forward("a", 1)
    stage_two("a", (-1, 1))
    for w in e: w.wait_recv()
    e = table_sends(ex.at[:, z], [device("z", s) for s in (1, 2, -1)])
    qy.forward()
    finish("a", 1)
    stage_two("a", (2,))
    for w in e: w.wait_recv()
    for w in weights: w.start()

    place = [((x + dx + 4) % 4, (z + dz + 4) % 4) for dx, dz in CHIPS]
    for n, (px, pz) in enumerate(place):
        for s in range(2):
            block = ex[px, pz, s].astype(F32)
            for q in range(24):
                rs[q, 2 * n + s:2 * n + s + 1, :] = block[q:q + 1]
    routes = [rs[k] for k in range(8)]
    probs = [rs[8 + k] + rs[16 + k] for k in range(8)]
    tri = (lax.broadcasted_iota(jnp.int32, (128, 128), 0) < lax.broadcasted_iota(jnp.int32, (128, 128), 1)).astype(F32).astype(BF)
    for e in range(2):
        name = (dp * 2 + e).astype(F32)
        member = jnp.zeros((32, 128), F32); weight = jnp.zeros((32, 128), F32)
        for k in range(8):
            hit = routes[k] == name
            member = member + jnp.where(hit, 1.0, 0.0)
            weight = weight + jnp.where(hit, probs[k], 0.0)
        before = nn(member.astype(BF), tri)
        offset = ((lax.broadcasted_iota(jnp.int32, (32, 128), 0) % 4) * 20).astype(F32)
        target = jnp.where(member > 0.5, before + offset, -1.0)
        for g in range(8):
            t4 = jnp.concatenate([target[g * 4 + i:g * 4 + i + 1] for i in range(4)], axis=1)
            w4 = jnp.concatenate([weight[g * 4 + i:g * 4 + i + 1] for i in range(4)], axis=1)
            oh = jnp.where(lax.broadcasted_iota(jnp.int32, (80, 512), 0).astype(F32) == t4, 1.0, 0.0)
            onehot[g, e * 80:(e + 1) * 80, :] = oh.astype(BF)
            prob[e, g * 80:(g + 1) * 80, :] = jnp.broadcast_to(jnp.sum(oh * w4, axis=1, keepdims=True), (80, 128))

    forward("a", 2, 0)
    qy.finish()
    keep.wait()
    stage_one("q")
    waited = set()
    def need(q, g):
        for key in CHIPS[2 * g:2 * g + 2]:
            for f, a, b in sets(q):
                if (f, key) not in waited:
                    waited.add((f, key))
                    sibs[(f,) + key].wait_recv()
    base = pl.multiple_of(y * 1024, 1024)
    def pack_own(g):
        need("a", g)
        v = jnp.concatenate([ga[px, pz].reshape(256, CA) for px, pz in place[2 * g:2 * g + 2]], axis=0)
        out = nn(onehot[g], v).astype(BF)
        rows = pl.ds(g * 80, 80)
        for e in range(2):
            xh[e, rows, pl.ds(base, HA)] = out[e * 80:(e + 1) * 80, :HA]
            xg[e, rows, pl.ds(base, GA)] = out[e * 80:(e + 1) * 80, HA:]
    class Slots:
        def __init__(self, g):
            self.g = g
            self.up = [send(v, v, device("y", 1)) for v in self.refs(y)]
            self.down = [send(v, v, device("y", -1)) for v in self.refs(y)]
        def refs(self, yy, es=pl.ds(0, 2)):
            at = pl.multiple_of(yy * 1024, 1024)
            rows = pl.ds(self.g * 80, 80)
            return xh.at[es, rows, pl.ds(at, HA)], xg.at[es, rows, pl.ds(at, GA)]
        def forward(self):
            for w in self.up: w.wait_recv()
            self.up2 = [send(v, v, device("y", 1)) for v in self.refs((y + 3) % 4, pl.ds(0, 1))]
            for w in self.down: w.wait_recv()
            self.down2 = [send(v, v, device("y", -1)) for v in self.refs((y + 1) % 4, pl.ds(1, 1))]
        def finish(self):
            for w in self.up2 + self.down2: w.wait_recv()
            for w in self.up + self.down + self.up2 + self.down2:
                w.wait_send()
                pending[:] = [q for q in pending if q is not w]
    def q_copies(g, yy):
        return [pltpu.make_async_copy(gq.at[px, pz, :, yy], qb.at[yy, i], qsem.at[yy, i])
                for i, (px, pz) in enumerate(place[2 * g:2 * g + 2])]
    def q_start(g):
        for yy in range(4):
            for w in q_copies(g, yy): w.start()
    def pack_rest(groups):
        for g in groups: need("q", g)
        q_start(groups[0])
        for g, after in zip(groups, groups[1:] + (None,)):
            for yy in range(4):
                for w in q_copies(g, yy): w.wait()
                out = nn(onehot[g], qb[yy].reshape(512, CQ)).astype(BF)
                rows = pl.ds(g * 80, 80)
                for e in range(2):
                    xh[e, rows, yy * 1024 + HA:(yy + 1) * 1024] = out[e * 80:(e + 1) * 80, :1024 - HA]
                    xg[e, rows, yy * 1024 + GA:(yy + 1) * 1024] = out[e * 80:(e + 1) * 80, 1024 - HA:]
                if after is not None:
                    for w in q_copies(after, yy): w.start()
    spans = ((0, 400), (400, 240))
    def units_in(h, e):
        first, count = spans[h]
        rows = pl.ds(first, count)
        part = pl.ds(0, count)
        @pl.loop(0, 4)
        def _(kk):
            cols = pl.ds(pl.multiple_of(kk * 1024, 1024), 1024)
            both = nn(xh[e, rows, cols], wgu[e, cols, :])
            last = nt(xg[e, rows, cols], wd[e, :, cols])
            @pl.when(kk == 0)
            def _():
                gu[part] = both
                back[part] = last
            @pl.when(kk > 0)
            def _():
                gu[part] += both
                back[part] += last
    def units_out(h, e):
        first, count = spans[h]
        rows = pl.ds(first, count)
        @pl.loop(0, count // 80)
        def _(r):
            here_rows = pl.ds(pl.multiple_of(r * 80, 16), 80)
            all_rows = pl.ds(pl.multiple_of(first + r * 80, 16), 80)
            gp = gu[here_rows, 0:384]; u = gu[here_rows, 384:768]; b = back[here_rows, :]
            sig = 1.0 / (1.0 + jnp.exp(-gp))
            act = gp * sig
            sprob[e, all_rows, :] = jnp.broadcast_to(jnp.sum(b * act * u, axis=1, keepdims=True), (80, 128))
            p = prob[e, all_rows, 0:1]
            ggu[here_rows, 0:384] = (b * u * sig * (1.0 + gp * (1.0 - sig)) * p).astype(BF)
            ggu[here_rows, 384:768] = (b * act * p).astype(BF)
        @pl.loop(0, 4)
        def _(kk):
            cols = pl.ds(pl.multiple_of(kk * 1024, 1024), 1024)
            xh[e, rows, cols] = nt(ggu[0:count], wgu[e, cols, :]).astype(BF)
        out_copies.append(pltpu.make_async_copy(xh.at[e, rows], ws_out.at[e, rows], wsem.at[3 + h * 2 + e]))
        out_copies[-1].start()

    out_copies = []
    oh_copy = pltpu.make_async_copy(onehot, oh_out, own_sem.at[2])
    oh_copy.start()
    S = {}
    forward("a", 2, -1)
    pack_own(0); S[0] = Slots(0)
    pack_own(1); S[1] = Slots(1)
    forward("a", 2, 1)
    pack_own(2); S[2] = Slots(2)
    pack_own(3)
    forward("a", 2, 2)
    for s in STEPS: finish("a", 2, s)
    for g in range(4, 8): pack_own(g)
    S[0].forward(); S[3] = Slots(3)
    S[1].forward(); S[4] = Slots(4)
    forward("q", 1)
    stage_two("q", (-1, 1))
    S[2].forward(); S[5] = Slots(5)
    forward("q", 2, 0)
    finish("q", 1)
    stage_two("q", (2,))
    S[3].forward(); S[6] = Slots(6)
    forward("q", 2, -1)
    pack_rest((0, 1))
    S[4].forward(); S[7] = Slots(7)
    forward("q", 2, 1)
    pack_rest((2, 3))
    finish("q", 2, 0)
    pack_rest((4,))
    for w in weights: w.wait()
    for g in range(5): S[g].finish()
    units_in(0, 0)
    S[5].forward()
    finish("q", 2, -1)
    forward("q", 2, 2)
    units_out(0, 0)
    S[6].forward()
    finish("q", 2, 1)
    units_in(0, 1)
    S[7].forward()
    finish("q", 2, 2)
    units_out(0, 1)
    pack_rest((5, 6, 7))
    for g in range(5, 8): S[g].finish()
    for e in range(2):
        units_in(1, e)
        units_out(1, e)

    for g in range(8):
        for e in range(2):
            oh = onehot[g, e * 80:(e + 1) * 80, :].astype(F32)
            row = jnp.sum(oh * sprob[e, g * 80:(g + 1) * 80, 0:1], axis=0, keepdims=True)
            for i in range(4):
                spt[e, g * 4 + i:g * 4 + i + 1, :] = row[:, i * 128:(i + 1) * 128]
    n0 = (dp * 2).astype(F32)
    line = lax.broadcasted_iota(jnp.int32, (32, 16, 128), 1)
    def routed(k):
        r = rs[k]
        return (jnp.where(r == n0, spt[0], 0.0) + jnp.where(r == n0 + 1.0, spt[1], 0.0))[:, None, :]
    for k in range(4):
        rr[:, :, k * 128:(k + 1) * 128] = (jnp.where(line == 0, routed(k), 0.0) + jnp.where(line == 1, routed(k + 4), 0.0)).astype(BF)
    rr_copy = pltpu.make_async_copy(rr, rr_out, own_sem.at[1])
    rr_copy.start()
    oh_copy.wait()
    for w in out_copies: w.wait()
    rr_copy.wait()
    for s in pending: s.wait_send()

def experts(hid, gra, routes, probs, wg, wu, wd):
    V=pltpu.VMEM
    A=pl.BlockSpec(memory_space=pl.ANY)
    N=7 + 4 + 2 * (40 + 32) + 64
    return pl.pallas_call(expert_kernel,
        out_shape=(jax.ShapeDtypeStruct((2,640,4096),BF), jax.ShapeDtypeStruct((8,160,512),BF), jax.ShapeDtypeStruct((32,16,512),BF), jax.ShapeDtypeStruct((4,4,2,4,128,CQ),BF)),
        in_specs=[pl.BlockSpec(memory_space=V)]*4+[A]*3, out_specs=(A,)*4,
        scratch_shapes=[V((2,4096,768),BF),V((2,384,4096),BF),
            V((2,640,4096),BF),V((2,640,4096),BF),V((4,4,2,128,CA),BF),V((128,CQ),BF),V((4,4,2,32,128),BF),V((24,32,128),F32),V((32,16,512),BF),
            V((8,160,512),BF),V((2,640,128),F32),V((2,640,128),F32),V((4,2,2,128,CQ),BF),
            V((400,768),F32),V((400,384),F32),V((400,768),BF),V((2,32,128),F32),
            pltpu.SemaphoreType.DMA((5,)),pltpu.SemaphoreType.DMA((7,)),pltpu.SemaphoreType.DMA((4,2)),
            pltpu.SemaphoreType.DMA((N,)),pltpu.SemaphoreType.DMA((N,))],
        compiler_params=pltpu.CompilerParams(collective_id=0, has_side_effects=True, vmem_limit_bytes=63*1024*1024),
    )(hid, gra, routes, probs, wg, wu, wd)[:3]

def return_kernel(ws_hbm, oh_hbm, rr_hbm, partner, swap_count, grad, router, ws, onehot, rr, y1, y2, red, pq, sq, lq, pa, sa, la, ly, lr, fin, inc,
                  in_sem, g_sem, send_sem, recv_sem):
    dp = lax.axis_index("dp"); y = lax.axis_index("tensor")
    x = dp // 8; z = (dp // 2) % 4; c = dp % 2
    here = {"x": x, "y": y, "z": z}
    def device(axis, step):
        if axis == "c":
            return {"dp": x * 8 + z * 2 + (1 - c), "tensor": y}
        at = dict(here)
        at[axis] = (at[axis] + step + 4) % 4
        return {"dp": at["x"] * 8 + at["z"] * 2 + c, "tensor": at["y"]}
    mates = []
    for bit in range(3):
        low = (dp // (1 << bit)) % 2
        mates.append({"dp": dp + (1 - 2 * low) * (1 << bit), "tensor": y})
    def g_copy(g):
        rows = pl.ds(g * 80, 80)
        return pltpu.make_async_copy(ws_hbm.at[:, rows], ws.at[:, rows], g_sem.at[g])
    small = [pltpu.make_async_copy(oh_hbm, onehot, in_sem.at[0]), pltpu.make_async_copy(rr_hbm, rr, in_sem.at[1])]
    for s in small: s.start()
    for g in reversed(range(8)): g_copy(g).start()
    barrier = pltpu.get_barrier_semaphore()
    partners = [device(a, s) for a in "xyz" for s in (1, -1)] + [device("y", 2)] + mates
    for p in partners:
        pl.semaphore_signal(barrier, inc=1, device_id=p, device_id_type=MESH)
    pl.semaphore_wait(barrier, len(partners))

    number = [0]
    pending = []
    def send(src, dst, to):
        n = number[0]; number[0] += 1
        copy = pltpu.make_async_remote_copy(src_ref=src, dst_ref=dst, send_sem=send_sem.at[n],
            recv_sem=recv_sem.at[n], device_id=to, device_id_type=MESH)
        copy.start()
        pending.append(copy)
        return copy
    def add(dst, *terms):
        if len(dst.shape) == 3:
            @pl.loop(0, dst.shape[0])
            def _(i):
                total = terms[0][i].astype(F32)
                for t in terms[1:]: total = total + t[i].astype(F32)
                dst[i] = total.astype(BF)
        else:
            total = terms[0][...].astype(F32)
            for t in terms[1:]: total = total + t[...].astype(F32)
            dst[...] = total.astype(BF)
    class Ring:
        def __init__(self, axis, land, far_up, far_down):
            self.axis, self.land = axis, land
            self.up1 = send(far_up, land[0], device(axis, 1))
            self.down1 = send(far_down, land[1], device(axis, -1))
        def middle(self, after, after_up, before, before_down):
            self.up1.wait_recv()
            add(after_up, after_up, self.land[0])
            self.up2 = send(after, self.land[2], device(self.axis, 1))
            self.down1.wait_recv()
            add(before_down, before_down, self.land[1])
            self.down2 = send(before, self.land[3], device(self.axis, -1))
        def finish(self, near):
            self.up2.wait_recv(); self.down2.wait_recv()
            add(near, near, self.land[2], self.land[3])

    def slot(g, k, es=pl.ds(0, 2)):
        at = pl.multiple_of(((y + k + 4) % 4) * 1024, 1024)
        return ws.at[es, pl.ds(g * 80, 80), pl.ds(at, RA)]
    Y = {}
    def y_start(g):
        Y[g] = Ring("y", (y1.at[g, pl.ds(0, 1)], y1.at[g, pl.ds(1, 1)], y2.at[g, 0], y2.at[g, 1]),
                    slot(g, 2, pl.ds(0, 1)), slot(g, 2, pl.ds(1, 1)))
    def y_middle(g):
        Y[g].middle(slot(g, 1), slot(g, 1, pl.ds(0, 1)), slot(g, -1), slot(g, -1, pl.ds(1, 1)))
    def y_finish(g):
        Y[g].finish(slot(g, 0))
    def spread(g):
        return onehot[g].astype(F32).T.astype(BF)
    sib = {}
    def combine_rest(g):
        oht = spread(g)
        for t in range(4):
            v = jnp.concatenate([ws[e, g * 80:(g + 1) * 80, t * 1024 + RA:(t + 1) * 1024] for e in range(2)], axis=0)
            out = nn(oht, v).astype(BF)
            for i in range(4):
                pq[i % 2, 2 * g + i // 2, t] = out[i * 128:(i + 1) * 128]
        for n in (2 * g + 1, 2 * g):
            sib["q", n] = send(pq.at[1 - c, n], sq.at[n], device("c", 0))
    def combine_own(g):
        oht = spread(g)
        at = pl.ds(pl.multiple_of(y * 1024, 1024), RA)
        v = jnp.concatenate([ws[e, g * 80:(g + 1) * 80, at] for e in range(2)], axis=0)
        out = nn(oht, v).astype(BF)
        for i in range(4):
            pa[i % 2, 2 * g + i // 2, 16:144] = out[i * 128:(i + 1) * 128]
            pa[i % 2, 2 * g + i // 2, 0:16] = rr[g * 4 + i]
        for n in (2 * g + 1, 2 * g):
            sib["a", n] = send(pa.at[1 - c, n], sa.at[n], device("c", 0))
    def merge(q, n):
        sib[q, n].wait_recv()
        if q == "q":
            add(pq.at[c, n], pq.at[c, n], sq.at[n])
        else:
            add(pa.at[c, n], pa.at[c, n], sa.at[n])
    def block(q, f, n, part="all"):
        if q == "q":
            ts = {"all": pl.ds(0, 4), "up": pl.ds(0, 2), "down": pl.ds(2, 2)}[part]
            return pq.at[c, n, ts, pl.ds(64 * f, 64)]
        first, count = {"all": ((0, 80), (80, 64)), "up": ((0, 48), (80, 32)), "down": ((48, 32), (112, 32))}[part][f]
        return pa.at[c, n, pl.ds(first, count)]
    def land(q, f, r):
        if q == "q":
            v = lq.at[f, r]
            return v.at[pl.ds(0, 2)], v.at[pl.ds(2, 2)], v.at[pl.ds(4, 4)], v.at[pl.ds(8, 4)]
        up, down = ((48, 32), (32, 32))[f]
        v = la.at[f, r]
        return v.at[pl.ds(0, up)], v.at[pl.ds(48, down)], v.at[pl.ds(80, up + down)], v.at[pl.ds(160, up + down)]
    R = {}
    def chip(f, s, k):
        return CHIPS.index((s, k) if f == 0 else (k, s))
    def start_one(q, s):
        for f in (0, 1):
            n = chip(f, s, 2)
            R[q, f, s] = Ring("zx"[f], land(q, f, STEPS.index(s)), block(q, f, n, "up"), block(q, f, n, "down"))
    def middle_one(q, s):
        for f in (0, 1):
            a, b = chip(f, s, 1), chip(f, s, -1)
            R[q, f, s].middle(block(q, f, a), block(q, f, a, "up"), block(q, f, b), block(q, f, b, "down"))
    def finish_one(q, s):
        for f in (0, 1): R[q, f, s].finish(block(q, f, chip(f, s, 0)))
    def start_two(q):
        for f in (0, 1):
            n = chip(f, 2, 0)
            R[q, f, "two"] = Ring("xz"[f], land(q, f, 4), block(q, f, n, "up"), block(q, f, n, "down"))
    def middle_two(q):
        for f in (0, 1):
            a, b = chip(f, 1, 0), chip(f, -1, 0)
            R[q, f, "two"].middle(block(q, f, a), block(q, f, a, "up"), block(q, f, b), block(q, f, b, "down"))
    def finish_two(q):
        for f in (0, 1): R[q, f, "two"].finish(block(q, f, 0))

    for s in small: s.wait()
    def group(g):
        g_copy(g).wait()
        y_start(g)
        combine_rest(g)
    def own(*gs):
        for g in gs:
            y_finish(g); combine_own(g)
    def merges(q, *ns):
        for n in ns: merge(q, n)
    group(7); group(6)
    merges("q", 15); start_one("q", 2)
    group(5)
    merges("q", 14, 13); start_one("q", 1)
    group(4)
    merges("q", 12, 11); start_one("q", -1)
    y_middle(7); group(3)
    merges("q", 10, 9); start_one("q", 0)
    y_middle(6); group(2)
    merges("q", 8); middle_one("q", 2)
    y_middle(5); group(1)
    merges("q", 7, 6); middle_one("q", 1)
    y_middle(4); group(0)
    merges("q", 5, 4, 3); middle_one("q", -1)
    own(7, 6)
    y_middle(3)
    merges("q", 2, 1, 0); middle_one("q", 0)
    y_middle(2)
    own(5, 4)
    finish_one("q", 2); start_two("q")
    merges("a", 15, 14, 13, 12, 11, 10, 9)
    for s in (2, 1, -1, 0): start_one("a", s)
    y_middle(1); y_middle(0)
    finish_one("q", 1); finish_one("q", -1); middle_two("q")
    merges("a", 8); middle_one("a", 2)
    own(3, 2, 1, 0)
    finish_one("q", 0)
    merges("a", 7, 6); middle_one("a", 1)
    merges("a", 5, 4, 3); middle_one("a", -1)
    merges("a", 2, 1, 0); middle_one("a", 0)
    finish_one("a", 2); start_two("a")
    finish_two("q")
    def rest(k, part=pl.ds(0, 128)):
        return pq.at[c, 0, (y + k + 4) % 4, part]
    lo, hi = pl.ds(0, 64), pl.ds(64, 64)
    last = Ring("y", (ly.at[pl.ds(0, 64)], ly.at[pl.ds(64, 64)], ly.at[pl.ds(128, 128)], ly.at[pl.ds(256, 128)]), rest(2, lo), rest(2, hi))
    finish_one("a", 1); finish_one("a", -1)
    middle_two("a")
    last.middle(rest(1), rest(1, lo), rest(-1), rest(-1, hi))
    finish_one("a", 0)
    finish_two("a")
    odds = [send(pa.at[c, 0, pl.ds(0, 16)], lr.at[i], device("y", s)) for i, s in enumerate((1, 2, -1))]
    fin[:, 0:RA] = pa[c, 0, 16:144]
    swaps = [send(fin.at[64:128, 0:RA], inc.at[b, :, 0:RA], mates[b]) for b in range(3)]
    last.finish(rest(0))
    fin[:, RA:1024] = pq[c, 0, y]
    swaps += [send(fin.at[64:128, RA:1024], inc.at[b, :, RA:1024], mates[b]) for b in range(3)]
    for o in odds: o.wait_recv()
    total = pa[c, 0, 0:16].astype(F32) + lr[0].astype(F32) + lr[1].astype(F32) + lr[2].astype(F32)
    table = jnp.concatenate([total[k // 4:k // 4 + 1, (k % 4) * 128:(k % 4 + 1) * 128] for k in range(8)], axis=0)
    router[...] = table.astype(BF)
    grad[0:64, :] = fin[0:64, :]
    for s in swaps: s.wait_recv()
    row = lax.broadcasted_iota(jnp.int32, (64, 1024), 0)
    kept = fin[64:128, :].astype(F32)
    taken = row >= 64 - swap_count[dp]
    apart = jnp.bitwise_xor(partner[dp], dp)
    for b in range(3):
        kept = jnp.where(taken & (apart == (1 << b)), inc[b].astype(F32), kept)
    grad[64:128, :] = kept.astype(BF)
    for s in pending: s.wait_send()

def returned(ws, oh, rr, partner, swap_count):
    V=pltpu.VMEM
    A=pl.BlockSpec(memory_space=pl.ANY)
    N=16 + 16 + 40 + 40 + 32 + 4 + 3 + 6
    return pl.pallas_call(return_kernel,
        out_shape=(jax.ShapeDtypeStruct((128,1024),BF),jax.ShapeDtypeStruct((8,128),BF)),
        in_specs=[A,A,A,pl.BlockSpec(memory_space=pltpu.SMEM),pl.BlockSpec(memory_space=pltpu.SMEM)],
        out_specs=(pl.BlockSpec(memory_space=V),pl.BlockSpec(memory_space=V)),
        scratch_shapes=[V((2,640,4096),BF),V((8,160,512),BF),V((32,16,RA),BF),
            V((8,2,80,RA),BF),V((8,2,2,80,RA),BF),V((8,128),F32),
            V((2,16,4,128,RQ),BF),V((16,4,128,RQ),BF),V((2,5,12,64,RQ),BF),
            V((2,16,144,RA),BF),V((16,144,RA),BF),V((2,5,240,RA),BF),
            V((384,RQ),BF),V((3,16,RA),BF),V((128,1024),BF),V((3,64,1024),BF),
            pltpu.SemaphoreType.DMA((2,)),pltpu.SemaphoreType.DMA((8,)),pltpu.SemaphoreType.DMA((N,)),pltpu.SemaphoreType.DMA((N,))],
        compiler_params=pltpu.CompilerParams(collective_id=1, has_side_effects=True, vmem_limit_bytes=63*1024*1024),
    )(ws, oh, rr, partner, swap_count)

def local(hidden, grad_out, routes, route_probs, w_gate, w_up, w_down, partner, swap_count):
    ws, oh, rr = experts(hidden, grad_out, routes.T, route_probs.T, w_gate, w_up, w_down)
    grad, router = returned(ws, oh, rr, partner, swap_count)
    return grad, router.T


def solution(mesh):
    placed = (
        P("dp", "tensor"),
        P("dp", "tensor"),
        P("dp", None),
        P("dp", None),
        P("dp", None, "tensor"),
        P("dp", None, "tensor"),
        P("dp", "tensor", None),
        P(),
        P(),
    )
    return jax.shard_map(
        local,
        mesh=mesh,
        in_specs=placed,
        out_specs=(P("dp", "tensor"), P("dp", None)),
        check_vma=False,
    )
```

```python
import functools
import jax
import jax.numpy as jnp
from jax import lax
from jax.experimental import pallas as pl
from jax.experimental.pallas import tpu as pltpu
from jax.sharding import PartitionSpec as P

MESH = pl.DeviceIdType.MESH
BF=jnp.bfloat16; F32=jnp.float32
HA=512
GA=512
CA=HA+GA
CQ=2048-CA
STEPS=(0,-1,1,2)
CHIPS=((0,0),(0,-1),(-1,0),(-1,-1),(0,1),(1,0),(-1,1),(1,-1),(1,1),(0,2),(2,0),(-1,2),(2,-1),(1,2),(2,1),(2,2))
RA=512
RQ=1024-RA

def nt(a,b): return lax.dot_general(a,b,(((1,),(1,)),((),())),preferred_element_type=F32)
def nn(a,b): return jnp.dot(a,b,preferred_element_type=F32)

def expert_kernel(hid, gra, routes_ref, probs_ref, wg_hbm, wu_hbm, wd_hbm, ws_out, oh_out, rr_out, gq, wgu, wd, xh, xg, ga, qo, ex, rs, rr, onehot, prob, sprob, qb,
                  gu, back, ggu, spt, own_sem, wsem, qsem, send_sem, recv_sem):
    dp = lax.axis_index("dp"); y = lax.axis_index("tensor")
    x = dp // 8; z = (dp // 2) % 4; c = dp % 2
    here = {"x": x, "y": y, "z": z}
    def device(axis, step):
        if axis == "c":
            return {"dp": x * 8 + z * 2 + (1 - c), "tensor": y}
        at = dict(here)
        at[axis] = (at[axis] + step + 4) % 4
        return {"dp": at["x"] * 8 + at["z"] * 2 + c, "tensor": at["y"]}
    barrier = pltpu.get_barrier_semaphore()
    partners = [device(a, s) for a in "xyz" for s in (1, -1)] + [device("x", 2), device("z", 2), device("c", 0)]
    for p in partners:
        pl.semaphore_signal(barrier, inc=1, device_id=p, device_id_type=MESH)
    probs = probs_ref[...]
    high = probs.astype(BF).astype(F32)
    ex[x, z, c] = jnp.concatenate([routes_ref[...].astype(F32), high, probs - high, jnp.zeros((8, 128), F32)], axis=0).astype(BF)
    ga[x, z, c, :, 0:HA] = hid[:, 0:HA]
    ga[x, z, c, :, HA:CA] = gra[:, 0:GA]
    qo[:, 0:1024 - HA] = hid[:, HA:1024]
    qo[:, 1024 - HA:CQ] = gra[:, GA:1024]
    keep = pltpu.make_async_copy(qo, gq.at[x, z, c, y], own_sem.at[0])
    keep.start()
    pl.semaphore_wait(barrier, len(partners))

    number = [0]
    pending = []
    def send(src, dst, to):
        n = number[0]; number[0] += 1
        copy = pltpu.make_async_remote_copy(src_ref=src, dst_ref=dst, send_sem=send_sem.at[n],
            recv_sem=recv_sem.at[n], device_id=to, device_id_type=MESH)
        copy.start()
        pending.append(copy)
        return copy
    def view(fam, at, part="all"):
        xx = pl.ds(0, 4) if at["x"] is None else at["x"]
        if fam in ("alo", "ahi"):
            first = 0 if fam == "alo" else 64
            first, count = {"all": (first, 64), "up": (first, 32), "down": (first + 32, 32)}[part]
            return ga.at[xx, at["z"], c, pl.ds(first, count)]
        if fam in ("qlo", "qhi"):
            ys = {"all": pl.ds(0, 4), "up": pl.ds(0, 2), "down": pl.ds(2, 2)}[part]
            return gq.at[xx, at["z"], c, ys, pl.ds(0 if fam == "qlo" else 64, 64)]
        rows = {"all": (0, 128), "up": (0, 64), "down": (64, 64)}[part]
        return gq.at[x, z, c, at["y"], pl.ds(*rows)]
    sibs = {}
    def to_sibling(fam, at, key):
        if key is None: return
        v = view(fam, at)
        sibs[(fam,) + key] = send(v, v, device("c", 0))
    def moved(at, axis, step):
        q = dict(at); q[axis] = (here[axis] + step + 4) % 4
        return q
    class Ring:
        def __init__(self, fam, axis, at, off, src=None):
            self.fam, self.axis, self.at, self.off = fam, axis, at, off
            v = view(fam, at)
            self.up = send(v if src is None else src, v, device(axis, 1))
            self.down = send(v if src is None else src, v, device(axis, -1))
        def key(self, step):
            if self.off is None: return None
            o = dict(self.off); o[self.axis] = step
            return (o["x"], o["z"])
        def forward(self):
            f, a = self.fam, self.axis
            before, after = moved(self.at, a, -1), moved(self.at, a, 1)
            self.up.wait_recv()
            v = view(f, before, "up")
            self.up2 = send(v, v, device(a, 1))
            to_sibling(f, before, self.key(-1))
            self.down.wait_recv()
            v = view(f, after, "down")
            self.down2 = send(v, v, device(a, -1))
            to_sibling(f, after, self.key(1))
        def finish(self):
            self.up2.wait_recv()
            self.down2.wait_recv()
            to_sibling(self.fam, moved(self.at, self.axis, 2), self.key(2))
    def sets(q):
        return ((q + "lo", "x", "z"), (q + "hi", "z", "x"))
    R = {}
    zero = {"x": 0, "z": 0}
    def stage_one(q):
        for f, a, b in sets(q): R[f, 1] = Ring(f, a, here, zero)
        for f, a, b in sets(q): R[f, 2, 0] = Ring(f, b, here, zero)
        for f, a, b in sets(q): to_sibling(f, here, (0, 0))
    def stage_two(q, steps):
        for f, a, b in sets(q):
            for s in steps:
                off = dict(zero); off[a] = s
                R[f, 2, s] = Ring(f, b, moved(here, a, s), off)
    def forward(q, *which):
        for f, a, b in sets(q): R[(f,) + which].forward()
    def finish(q, *which):
        for f, a, b in sets(q): R[(f,) + which].finish()

    def table_sends(v, to):
        return [send(v, v, d) for d in to]
    e = table_sends(ex.at[x, z, c], [device("c", 0)])
    qy = Ring("Q", "y", here, None, qo)
    stage_one("a")
    weights = [pltpu.make_async_copy(a, b, wsem.at[i]) for i,(a,b) in enumerate(((wg_hbm, wgu.at[:, :, pl.ds(0, 384)]), (wu_hbm, wgu.at[:, :, pl.ds(384, 384)]), (wd_hbm, wd)))]
    for w in e: w.wait_recv()
    e = table_sends(ex.at[x, z], [device("x", s) for s in (1, 2, -1)])
    forward("a", 1)
    stage_two("a", (-1, 1))
    for w in e: w.wait_recv()
    e = table_sends(ex.at[:, z], [device("z", s) for s in (1, 2, -1)])
    qy.forward()
    finish("a", 1)
    stage_two("a", (2,))
    qy.finish()
    keep.wait()
    stage_one("q")
    for w in e: w.wait_recv()
    for w in weights: w.start()

    place = [((x + dx + 4) % 4, (z + dz + 4) % 4) for dx, dz in CHIPS]
    for n, (px, pz) in enumerate(place):
        for s in range(2):
            block = ex[px, pz, s].astype(F32)
            for q in range(24):
                rs[q, 2 * n + s:2 * n + s + 1, :] = block[q:q + 1]
    routes = [rs[k] for k in range(8)]
    probs = [rs[8 + k] + rs[16 + k] for k in range(8)]
    tri = (lax.broadcasted_iota(jnp.int32, (128, 128), 0) < lax.broadcasted_iota(jnp.int32, (128, 128), 1)).astype(F32).astype(BF)
    for e in range(2):
        name = (dp * 2 + e).astype(F32)
        member = jnp.zeros((32, 128), F32); weight = jnp.zeros((32, 128), F32)
        for k in range(8):
            hit = routes[k] == name
            member = member + jnp.where(hit, 1.0, 0.0)
            weight = weight + jnp.where(hit, probs[k], 0.0)
        before = nn(member.astype(BF), tri)
        offset = ((lax.broadcasted_iota(jnp.int32, (32, 128), 0) % 4) * 20).astype(F32)
        target = jnp.where(member > 0.5, before + offset, -1.0)
        for g in range(8):
            t4 = jnp.concatenate([target[g * 4 + i:g * 4 + i + 1] for i in range(4)], axis=1)
            w4 = jnp.concatenate([weight[g * 4 + i:g * 4 + i + 1] for i in range(4)], axis=1)
            oh = jnp.where(lax.broadcasted_iota(jnp.int32, (80, 512), 0).astype(F32) == t4, 1.0, 0.0)
            onehot[g, e * 80:(e + 1) * 80, :] = oh.astype(BF)
            prob[e, g * 80:(g + 1) * 80, :] = jnp.broadcast_to(jnp.sum(oh * w4, axis=1, keepdims=True), (80, 128))

    forward("a", 2, 0)
    waited = set()
    def need(q, g):
        for key in CHIPS[2 * g:2 * g + 2]:
            for f, a, b in sets(q):
                if (f, key) not in waited:
                    waited.add((f, key))
                    sibs[(f,) + key].wait_recv()
    base = pl.multiple_of(y * 1024, 1024)
    def pack_own(g):
        need("a", g)
        v = jnp.concatenate([ga[px, pz].reshape(256, CA) for px, pz in place[2 * g:2 * g + 2]], axis=0)
        out = nn(onehot[g], v).astype(BF)
        rows = pl.ds(g * 80, 80)
        for e in range(2):
            xh[e, rows, pl.ds(base, HA)] = out[e * 80:(e + 1) * 80, :HA]
            xg[e, rows, pl.ds(base, GA)] = out[e * 80:(e + 1) * 80, HA:]
    class Slots:
        def __init__(self, g):
            self.g = g
            self.up = [send(v, v, device("y", 1)) for v in self.refs(y)]
            self.down = [send(v, v, device("y", -1)) for v in self.refs(y)]
        def refs(self, yy, es=pl.ds(0, 2)):
            at = pl.multiple_of(yy * 1024, 1024)
            rows = pl.ds(self.g * 80, 80)
            return xh.at[es, rows, pl.ds(at, HA)], xg.at[es, rows, pl.ds(at, GA)]
        def forward(self):
            for w in self.up: w.wait_recv()
            self.up2 = [send(v, v, device("y", 1)) for v in self.refs((y + 3) % 4, pl.ds(0, 1))]
            for w in self.down: w.wait_recv()
            self.down2 = [send(v, v, device("y", -1)) for v in self.refs((y + 1) % 4, pl.ds(1, 1))]
        def finish(self):
            for w in self.up2 + self.down2: w.wait_recv()
            for w in self.up + self.down + self.up2 + self.down2:
                w.wait_send()
                pending[:] = [q for q in pending if q is not w]
    def q_copies(g, yy):
        return [pltpu.make_async_copy(gq.at[px, pz, :, yy], qb.at[yy, i], qsem.at[yy, i])
                for i, (px, pz) in enumerate(place[2 * g:2 * g + 2])]
    def q_start(g):
        for yy in range(4):
            for w in q_copies(g, yy): w.start()
    def pack_rest(groups):
        for g in groups: need("q", g)
        q_start(groups[0])
        for g, after in zip(groups, groups[1:] + (None,)):
            for yy in range(4):
                for w in q_copies(g, yy): w.wait()
                out = nn(onehot[g], qb[yy].reshape(512, CQ)).astype(BF)
                rows = pl.ds(g * 80, 80)
                for e in range(2):
                    xh[e, rows, yy * 1024 + HA:(yy + 1) * 1024] = out[e * 80:(e + 1) * 80, :1024 - HA]
                    xg[e, rows, yy * 1024 + GA:(yy + 1) * 1024] = out[e * 80:(e + 1) * 80, 1024 - HA:]
                if after is not None:
                    for w in q_copies(after, yy): w.start()
    spans = ((0, 400), (400, 240))
    def units_in(h, e):
        first, count = spans[h]
        rows = pl.ds(first, count)
        part = pl.ds(0, count)
        @pl.loop(0, 4)
        def _(kk):
            cols = pl.ds(pl.multiple_of(kk * 1024, 1024), 1024)
            both = nn(xh[e, rows, cols], wgu[e, cols, :])
            last = nt(xg[e, rows, cols], wd[e, :, cols])
            @pl.when(kk == 0)
            def _():
                gu[part] = both
                back[part] = last
            @pl.when(kk > 0)
            def _():
                gu[part] += both
                back[part] += last
    def units_out(h, e):
        first, count = spans[h]
        rows = pl.ds(first, count)
        @pl.loop(0, count // 80)
        def _(r):
            here_rows = pl.ds(pl.multiple_of(r * 80, 16), 80)
            all_rows = pl.ds(pl.multiple_of(first + r * 80, 16), 80)
            gp = gu[here_rows, 0:384]; u = gu[here_rows, 384:768]; b = back[here_rows, :]
            sig = 1.0 / (1.0 + jnp.exp(-gp))
            act = gp * sig
            sprob[e, all_rows, :] = jnp.broadcast_to(jnp.sum(b * act * u, axis=1, keepdims=True), (80, 128))
            p = prob[e, all_rows, 0:1]
            ggu[here_rows, 0:384] = (b * u * sig * (1.0 + gp * (1.0 - sig)) * p).astype(BF)
            ggu[here_rows, 384:768] = (b * act * p).astype(BF)
        @pl.loop(0, 4)
        def _(kk):
            cols = pl.ds(pl.multiple_of(kk * 1024, 1024), 1024)
            xh[e, rows, cols] = nt(ggu[0:count], wgu[e, cols, :]).astype(BF)
        out_copies.append(pltpu.make_async_copy(xh.at[e, rows], ws_out.at[e, rows], wsem.at[3 + h * 2 + e]))
        out_copies[-1].start()

    out_copies = []
    oh_copy = pltpu.make_async_copy(onehot, oh_out, own_sem.at[2])
    oh_copy.start()
    S = {}
    forward("a", 2, -1)
    pack_own(0); S[0] = Slots(0)
    pack_own(1); S[1] = Slots(1)
    forward("a", 2, 1)
    pack_own(2); S[2] = Slots(2)
    pack_own(3)
    forward("a", 2, 2)
    for s in STEPS: finish("a", 2, s)
    for g in range(4, 8): pack_own(g)
    S[0].forward(); S[3] = Slots(3)
    S[1].forward(); S[4] = Slots(4)
    forward("q", 1)
    stage_two("q", (-1, 1))
    S[2].forward(); S[5] = Slots(5)
    forward("q", 2, 0)
    finish("q", 1)
    stage_two("q", (2,))
    S[3].forward(); S[6] = Slots(6)
    forward("q", 2, -1)
    pack_rest((0, 1))
    S[4].forward(); S[7] = Slots(7)
    forward("q", 2, 1)
    pack_rest((2, 3))
    finish("q", 2, 0)
    pack_rest((4,))
    for w in weights: w.wait()
    for g in range(5): S[g].finish()
    units_in(0, 0)
    S[5].forward()
    finish("q", 2, -1)
    forward("q", 2, 2)
    units_out(0, 0)
    S[6].forward()
    finish("q", 2, 1)
    units_in(0, 1)
    S[7].forward()
    finish("q", 2, 2)
    units_out(0, 1)
    pack_rest((5, 6, 7))
    for g in range(5, 8): S[g].finish()
    for e in range(2):
        units_in(1, e)
        units_out(1, e)

    for g in range(8):
        for e in range(2):
            oh = onehot[g, e * 80:(e + 1) * 80, :].astype(F32)
            row = jnp.sum(oh * sprob[e, g * 80:(g + 1) * 80, 0:1], axis=0, keepdims=True)
            for i in range(4):
                spt[e, g * 4 + i:g * 4 + i + 1, :] = row[:, i * 128:(i + 1) * 128]
    n0 = (dp * 2).astype(F32)
    line = lax.broadcasted_iota(jnp.int32, (32, 16, 128), 1)
    def routed(k):
        r = rs[k]
        return (jnp.where(r == n0, spt[0], 0.0) + jnp.where(r == n0 + 1.0, spt[1], 0.0))[:, None, :]
    for k in range(4):
        rr[:, :, k * 128:(k + 1) * 128] = (jnp.where(line == 0, routed(k), 0.0) + jnp.where(line == 1, routed(k + 4), 0.0)).astype(BF)
    rr_copy = pltpu.make_async_copy(rr, rr_out, own_sem.at[1])
    rr_copy.start()
    oh_copy.wait()
    for w in out_copies: w.wait()
    rr_copy.wait()
    for s in pending: s.wait_send()

def experts(hid, gra, routes, probs, wg, wu, wd):
    V=pltpu.VMEM
    A=pl.BlockSpec(memory_space=pl.ANY)
    N=7 + 4 + 2 * (40 + 32) + 64
    return pl.pallas_call(expert_kernel,
        out_shape=(jax.ShapeDtypeStruct((2,640,4096),BF), jax.ShapeDtypeStruct((8,160,512),BF), jax.ShapeDtypeStruct((32,16,512),BF), jax.ShapeDtypeStruct((4,4,2,4,128,CQ),BF)),
        in_specs=[pl.BlockSpec(memory_space=V)]*4+[A]*3, out_specs=(A,)*4,
        scratch_shapes=[V((2,4096,768),BF),V((2,384,4096),BF),
            V((2,640,4096),BF),V((2,640,4096),BF),V((4,4,2,128,CA),BF),V((128,CQ),BF),V((4,4,2,32,128),BF),V((24,32,128),F32),V((32,16,512),BF),
            V((8,160,512),BF),V((2,640,128),F32),V((2,640,128),F32),V((4,2,2,128,CQ),BF),
            V((400,768),F32),V((400,384),F32),V((400,768),BF),V((2,32,128),F32),
            pltpu.SemaphoreType.DMA((5,)),pltpu.SemaphoreType.DMA((7,)),pltpu.SemaphoreType.DMA((4,2)),
            pltpu.SemaphoreType.DMA((N,)),pltpu.SemaphoreType.DMA((N,))],
        compiler_params=pltpu.CompilerParams(collective_id=0, has_side_effects=True, vmem_limit_bytes=63*1024*1024),
    )(hid, gra, routes, probs, wg, wu, wd)[:3]

def return_kernel(ws_hbm, oh_hbm, rr_hbm, partner, swap_count, grad, router, ws, onehot, rr, y1, y2, red, pq, sq, lq, pa, sa, la, ly, lr, fin, inc,
                  in_sem, g_sem, send_sem, recv_sem):
    dp = lax.axis_index("dp"); y = lax.axis_index("tensor")
    x = dp // 8; z = (dp // 2) % 4; c = dp % 2
    here = {"x": x, "y": y, "z": z}
    def device(axis, step):
        if axis == "c":
            return {"dp": x * 8 + z * 2 + (1 - c), "tensor": y}
        at = dict(here)
        at[axis] = (at[axis] + step + 4) % 4
        return {"dp": at["x"] * 8 + at["z"] * 2 + c, "tensor": at["y"]}
    mates = []
    for bit in range(3):
        low = (dp // (1 << bit)) % 2
        mates.append({"dp": dp + (1 - 2 * low) * (1 << bit), "tensor": y})
    def g_copy(g):
        rows = pl.ds(g * 80, 80)
        return pltpu.make_async_copy(ws_hbm.at[:, rows], ws.at[:, rows], g_sem.at[g])
    small = [pltpu.make_async_copy(oh_hbm, onehot, in_sem.at[0]), pltpu.make_async_copy(rr_hbm, rr, in_sem.at[1])]
    for s in small: s.start()
    for g in reversed(range(8)): g_copy(g).start()
    barrier = pltpu.get_barrier_semaphore()
    partners = [device(a, s) for a in "xyz" for s in (1, -1)] + [device("y", 2), device("x", 2)] + mates
    for p in partners:
        pl.semaphore_signal(barrier, inc=1, device_id=p, device_id_type=MESH)
    pl.semaphore_wait(barrier, len(partners))

    number = [0]
    pending = []
    def send(src, dst, to):
        n = number[0]; number[0] += 1
        copy = pltpu.make_async_remote_copy(src_ref=src, dst_ref=dst, send_sem=send_sem.at[n],
            recv_sem=recv_sem.at[n], device_id=to, device_id_type=MESH)
        copy.start()
        pending.append(copy)
        return copy
    def add(dst, *terms):
        if len(dst.shape) == 3:
            @pl.loop(0, dst.shape[0])
            def _(i):
                total = terms[0][i].astype(F32)
                for t in terms[1:]: total = total + t[i].astype(F32)
                dst[i] = total.astype(BF)
        else:
            total = terms[0][...].astype(F32)
            for t in terms[1:]: total = total + t[...].astype(F32)
            dst[...] = total.astype(BF)
    class Ring:
        def __init__(self, axis, land, far_up, far_down):
            self.axis, self.land = axis, land
            self.up1 = send(far_up, land[0], device(axis, 1))
            self.down1 = send(far_down, land[1], device(axis, -1))
        def middle(self, after, after_up, before, before_down):
            self.up1.wait_recv()
            add(after_up, after_up, self.land[0])
            self.up2 = send(after, self.land[2], device(self.axis, 1))
            self.down1.wait_recv()
            add(before_down, before_down, self.land[1])
            self.down2 = send(before, self.land[3], device(self.axis, -1))
        def finish(self, near):
            self.up2.wait_recv(); self.down2.wait_recv()
            add(near, near, self.land[2], self.land[3])

    def slot(g, k, es=pl.ds(0, 2)):
        at = pl.multiple_of(((y + k + 4) % 4) * 1024, 1024)
        return ws.at[es, pl.ds(g * 80, 80), pl.ds(at, RA)]
    Y = {}
    def y_start(g):
        Y[g] = Ring("y", (y1.at[g, pl.ds(0, 1)], y1.at[g, pl.ds(1, 1)], y2.at[g, 0], y2.at[g, 1]),
                    slot(g, 2, pl.ds(0, 1)), slot(g, 2, pl.ds(1, 1)))
    def y_middle(g):
        Y[g].middle(slot(g, 1), slot(g, 1, pl.ds(0, 1)), slot(g, -1), slot(g, -1, pl.ds(1, 1)))
    def y_finish(g):
        Y[g].finish(slot(g, 0))
    def spread(g):
        return onehot[g].astype(F32).T.astype(BF)
    sib = {}
    def combine_rest(g):
        oht = spread(g)
        for t in range(4):
            v = jnp.concatenate([ws[e, g * 80:(g + 1) * 80, t * 1024 + RA:(t + 1) * 1024] for e in range(2)], axis=0)
            out = nn(oht, v).astype(BF)
            for i in range(4):
                pq[i % 2, 2 * g + i // 2, t] = out[i * 128:(i + 1) * 128]
        for n in (2 * g + 1, 2 * g):
            sib["q", n] = send(pq.at[1 - c, n], sq.at[n], device("c", 0))
    def combine_own(g):
        oht = spread(g)
        at = pl.ds(pl.multiple_of(y * 1024, 1024), RA)
        v = jnp.concatenate([ws[e, g * 80:(g + 1) * 80, at] for e in range(2)], axis=0)
        out = nn(oht, v).astype(BF)
        for i in range(4):
            pa[i % 2, 2 * g + i // 2, 16:144] = out[i * 128:(i + 1) * 128]
            pa[i % 2, 2 * g + i // 2, 0:16] = rr[g * 4 + i]
        for n in (2 * g + 1, 2 * g):
            sib["a", n] = send(pa.at[1 - c, n], sa.at[n], device("c", 0))
    def merge(q, n):
        sib[q, n].wait_recv()
        if q == "q":
            add(pq.at[c, n], pq.at[c, n], sq.at[n])
        else:
            add(pa.at[c, n], pa.at[c, n], sa.at[n])
    def block(q, f, n, part="all"):
        if q == "q":
            ts = {"all": pl.ds(0, 4), "up": pl.ds(0, 2), "down": pl.ds(2, 2)}[part]
            return pq.at[c, n, ts, pl.ds(64 * f, 64)]
        first, count = {"all": ((0, 80), (80, 64)), "up": ((0, 48), (80, 32)), "down": ((48, 32), (112, 32))}[part][f]
        return pa.at[c, n, pl.ds(first, count)]
    def land(q, f, r):
        if q == "q":
            v = lq.at[f, r]
            return v.at[pl.ds(0, 2)], v.at[pl.ds(2, 2)], v.at[pl.ds(4, 4)], v.at[pl.ds(8, 4)]
        up, down = ((48, 32), (32, 32))[f]
        v = la.at[f, r]
        return v.at[pl.ds(0, up)], v.at[pl.ds(48, down)], v.at[pl.ds(80, up + down)], v.at[pl.ds(160, up + down)]
    R = {}
    def chip(f, s, k):
        return CHIPS.index((s, k) if f == 0 else (k, s))
    def start_one(q, s):
        for f in (0, 1):
            n = chip(f, s, 2)
            R[q, f, s] = Ring("zx"[f], land(q, f, STEPS.index(s)), block(q, f, n, "up"), block(q, f, n, "down"))
    def middle_one(q, s):
        for f in (0, 1):
            a, b = chip(f, s, 1), chip(f, s, -1)
            R[q, f, s].middle(block(q, f, a), block(q, f, a, "up"), block(q, f, b), block(q, f, b, "down"))
    def finish_one(q, s):
        for f in (0, 1): R[q, f, s].finish(block(q, f, chip(f, s, 0)))
    def start_two(q):
        for f in (0, 1):
            n = chip(f, 2, 0)
            R[q, f, "two"] = Ring("xz"[f], land(q, f, 4), block(q, f, n, "up"), block(q, f, n, "down"))
    def middle_two(q):
        for f in (0, 1):
            a, b = chip(f, 1, 0), chip(f, -1, 0)
            R[q, f, "two"].middle(block(q, f, a), block(q, f, a, "up"), block(q, f, b), block(q, f, b, "down"))
    def finish_two(q):
        for f in (0, 1): R[q, f, "two"].finish(block(q, f, 0))

    def direct_land(f, s):
        return la.at[f, 4, pl.ds(80 * (2, 1, -1).index(s), (80, 64)[f])]
    def direct(s):
        for f in (0, 1):
            R["direct", f, s] = send(block("a", f, chip(f, s, 0)), direct_land(f, s), device("xz"[f], s))
    for s in small: s.wait()
    def group(g):
        g_copy(g).wait()
        y_start(g)
        combine_rest(g)
    def own(*gs):
        for g in gs:
            y_finish(g); combine_own(g)
    def merges(q, *ns):
        for n in ns: merge(q, n)
    group(7); group(6)
    merges("q", 15); start_one("q", 2)
    group(5)
    merges("q", 14, 13); start_one("q", 1)
    group(4)
    merges("q", 12, 11); start_one("q", -1)
    y_middle(7); group(3)
    merges("q", 10, 9); start_one("q", 0)
    y_middle(6); group(2)
    merges("q", 8); middle_one("q", 2)
    y_middle(5); group(1)
    merges("q", 7, 6); middle_one("q", 1)
    y_middle(4); group(0)
    merges("q", 5, 4, 3); middle_one("q", -1)
    own(7, 6)
    y_middle(3)
    merges("q", 2, 1, 0); middle_one("q", 0)
    y_middle(2)
    own(5, 4)
    finish_one("q", 2); start_two("q")
    merges("a", 15, 14, 13, 12, 11, 10, 9)
    for s in (2, 1, -1, 0): start_one("a", s)
    y_middle(1); y_middle(0)
    finish_one("q", 1); finish_one("q", -1); middle_two("q")
    merges("a", 8); middle_one("a", 2)
    own(3, 2, 1, 0)
    finish_one("q", 0)
    merges("a", 7, 6); middle_one("a", 1)
    merges("a", 5, 4, 3); middle_one("a", -1)
    merges("a", 2, 1, 0); middle_one("a", 0)
    finish_one("a", 2); direct(2)
    finish_two("q")
    def rest(k, part=pl.ds(0, 128)):
        return pq.at[c, 0, (y + k + 4) % 4, part]
    last = [send(rest(k), ly.at[pl.ds(128 * i, 128)], device("y", k)) for i, k in enumerate((2, 1, -1))]
    finish_one("a", 1); direct(1)
    finish_one("a", -1); direct(-1)
    finish_one("a", 0)
    for f in (0, 1):
        near = block("a", f, 0)
        for s in (2, 1, -1): R["direct", f, s].wait_recv()
        add(near, near, *(direct_land(f, s) for s in (2, 1, -1)))
    odds = [send(pa.at[c, 0, pl.ds(0, 16)], lr.at[i], device("y", s)) for i, s in enumerate((1, 2, -1))]
    fin[:, 0:RA] = pa[c, 0, 16:144]
    swaps = [send(fin.at[64:128, 0:RA], inc.at[b, :, 0:RA], mates[b]) for b in range(3)]
    for w in last: w.wait_recv()
    fin[:, RA:1024] = (pq[c, 0, y].astype(F32) + ly[0:128].astype(F32) + ly[128:256].astype(F32) + ly[256:384].astype(F32)).astype(BF)
    swaps += [send(fin.at[64:128, RA:1024], inc.at[b, :, RA:1024], mates[b]) for b in range(3)]
    for o in odds: o.wait_recv()
    total = pa[c, 0, 0:16].astype(F32) + lr[0].astype(F32) + lr[1].astype(F32) + lr[2].astype(F32)
    table = jnp.concatenate([total[k // 4:k // 4 + 1, (k % 4) * 128:(k % 4 + 1) * 128] for k in range(8)], axis=0)
    router[...] = table.astype(BF)
    grad[0:64, :] = fin[0:64, :]
    for s in swaps: s.wait_recv()
    row = lax.broadcasted_iota(jnp.int32, (64, 1024), 0)
    kept = fin[64:128, :].astype(F32)
    taken = row >= 64 - swap_count[dp]
    apart = jnp.bitwise_xor(partner[dp], dp)
    for b in range(3):
        kept = jnp.where(taken & (apart == (1 << b)), inc[b].astype(F32), kept)
    grad[64:128, :] = kept.astype(BF)
    for s in pending: s.wait_send()

def returned(ws, oh, rr, partner, swap_count):
    V=pltpu.VMEM
    A=pl.BlockSpec(memory_space=pl.ANY)
    N=16 + 16 + 40 + 40 + 32 + 4 + 3 + 6
    return pl.pallas_call(return_kernel,
        out_shape=(jax.ShapeDtypeStruct((128,1024),BF),jax.ShapeDtypeStruct((8,128),BF)),
        in_specs=[A,A,A,pl.BlockSpec(memory_space=pltpu.SMEM),pl.BlockSpec(memory_space=pltpu.SMEM)],
        out_specs=(pl.BlockSpec(memory_space=V),pl.BlockSpec(memory_space=V)),
        scratch_shapes=[V((2,640,4096),BF),V((8,160,512),BF),V((32,16,RA),BF),
            V((8,2,80,RA),BF),V((8,2,2,80,RA),BF),V((8,128),F32),
            V((2,16,4,128,RQ),BF),V((16,4,128,RQ),BF),V((2,5,12,64,RQ),BF),
            V((2,16,144,RA),BF),V((16,144,RA),BF),V((2,5,240,RA),BF),
            V((384,RQ),BF),V((3,16,RA),BF),V((128,1024),BF),V((3,64,1024),BF),
            pltpu.SemaphoreType.DMA((2,)),pltpu.SemaphoreType.DMA((8,)),pltpu.SemaphoreType.DMA((N,)),pltpu.SemaphoreType.DMA((N,))],
        compiler_params=pltpu.CompilerParams(collective_id=1, has_side_effects=True, vmem_limit_bytes=63*1024*1024),
    )(ws, oh, rr, partner, swap_count)

def local(hidden, grad_out, routes, route_probs, w_gate, w_up, w_down, partner, swap_count):
    ws, oh, rr = experts(hidden, grad_out, routes.T, route_probs.T, w_gate, w_up, w_down)
    grad, router = returned(ws, oh, rr, partner, swap_count)
    return grad, router.T


def solution(mesh):
    placed = (
        P("dp", "tensor"),
        P("dp", "tensor"),
        P("dp", None),
        P("dp", None),
        P("dp", None, "tensor"),
        P("dp", None, "tensor"),
        P("dp", "tensor", None),
        P(),
        P(),
    )
    return jax.shard_map(
        local,
        mesh=mesh,
        in_specs=placed,
        out_specs=(P("dp", "tensor"), P("dp", None)),
        check_vma=False,
    )
```
